128 devices in a mesh: tok: 4 (over y), vocab: 32 (over x, z, core).
Axes of the slice: x: 4, y: 4, z: 4, core: 2. Of those that a mesh axis runs over, the one named last changes fastest.
Arguments:
- teacher_logits: bfloat16 [512, 131072], P('tok', 'vocab'), may hold values from -18 to 240
- hidden: bfloat16 [512, 4608], P('tok'), may hold values from -6 to 6
- new_head: bfloat16 [4608, 131072], P(None, ('tok', 'vocab')), may hold values from -0.26516504 to 0.26516504
- labels: int32 [512], replicated, may hold values from 0 to 131071
- map_target: int32 [1024, 4], P('vocab'), may hold values from 0 to 1023, as said below
- map_weight: bfloat16 [1024, 4, 128, 128], P('vocab'), may hold values from 0 to 0.017578125, as said below
Outputs:
- loss: float32 [512], P('tok')
- head_grad: bfloat16 [4608, 131072], P(None, ('tok', 'vocab'))
The draws below stay inside these ranges and needn't reach their ends.
Inputs may be any that keep to these rules, and one draw needn't show every extreme that they name: `map_target`: values are ids of new blocks; new block b belongs to the device at index b // 8 of tok and vocab together, tok first. Of the 128 entries of one vocab index, at most 2 belong to one device, and some device gets exactly 2. `map_weight`: entries are non-negative.
All inputs are finite; a program needn't handle non-finite values.
Results may differ from the reference program's by a relative error of at most 0.001.
The reference program's roundings to bfloat16 on the way count: a program that leaves them out, or rounds other values in their place, can miss the bound.
Values may be sent and summed in bfloat16 or wider, within the bound.
A program may use at most 128 MiB of HBM per device.

```python
import math
import jax
import jax.numpy as jnp
import numpy as np
from jax import lax

D = 4608
VN_DEV = 1024
BLK = 128
FAN = 4
TOKENS = 512
V_OLD = 131072
V_NEW = 131072
OLD_BLOCKS = 32
OB_ALL = 1024
NEW_BLOCKS = 1024
CAP = 2
N_TOK = 4
N_VOCAB = 32


def draw_hidden(key, part):
    key = jax.random.fold_in(key, 11)
    rows = jnp.clip(jax.random.normal(jax.random.fold_in(key, 1), (TOKENS, D), jnp.float32), -6.0, 6.0)
    return rows.astype(jnp.bfloat16)


def draw_new_head(key, part):
    key = jax.random.fold_in(key, 12)
    spread = 3.0 * D ** (-0.5)
    weights = jnp.clip(jax.random.normal(jax.random.fold_in(key, 1), (D, V_NEW), jnp.float32), -6.0, 6.0) * spread
    return weights.astype(jnp.bfloat16)


def draw_teacher_logits(key, part):
    key = jax.random.fold_in(key, 13)
    values = jnp.clip(3.0 * jax.random.normal(jax.random.fold_in(key, 1), (TOKENS, V_OLD), jnp.float32), -18.0, 18.0)
    return values.astype(jnp.bfloat16)


def draw_map_weight(key, part):
    key = jax.random.fold_in(key, 14)
    uniform_part = jax.random.uniform(key, (OB_ALL, FAN, BLK, BLK), jnp.float32)
    diagonal = (jnp.arange(BLK)[:, None] == jnp.arange(BLK)[None, :]).astype(jnp.float32)
    return ((uniform_part + 8.0 * diagonal) * (1.0 / (FAN * BLK))).astype(jnp.bfloat16)


def shard_targets(key):
    entries = OLD_BLOCKS * FAN
    order = jax.random.permutation(jax.random.fold_in(key, 1), N_TOK * N_VOCAB)
    index = jnp.arange(entries, dtype=jnp.int32)
    groups = jnp.where(index < entries - 2, index // CAP, entries // CAP + index - (entries - 2))
    owners = order[groups]
    shuffle = jax.random.permutation(jax.random.fold_in(key, 2), entries)
    owners = owners[shuffle]
    within = jax.random.randint(jax.random.fold_in(key, 3), (entries,), 0, VN_DEV // BLK)
    return (owners * (VN_DEV // BLK) + within).astype(jnp.int32).reshape(OLD_BLOCKS, FAN)


def draw_map_target(key, part):
    key = jax.random.fold_in(key, 15)
    shard_keys = jax.vmap(lambda number: jax.random.fold_in(key, number))(jnp.arange(N_VOCAB))
    return jax.vmap(shard_targets)(shard_keys).reshape(OB_ALL, FAN)


def with_ends(values, own_key, smallest, largest):
    longest = values.shape.index(max(values.shape))
    spots = []
    for shift in (0, 1):
        where = [jax.random.randint(jax.random.fold_in(own_key, axis), (), 0, length) for axis, length in enumerate(values.shape)]
        where[longest] = (where[longest] + shift) % values.shape[longest]
        spots.append(tuple(where))
    return values.at[spots[0]].set(smallest).at[spots[1]].set(largest)


def ranked_wide(own_key, shape, count, lean):
    portions = [min(1 << octave, count + 1 - (1 << octave)) * (1 << 20) // math.isqrt((1 << octave) ** lean) + 1 for octave in range((count + 1).bit_length()) if 1 << octave <= count]
    width = 1 + sum(portions) // (1 << 30)
    table = np.cumsum(np.array([max(1, weight // width) for weight in portions]))
    pick = jax.random.randint(jax.random.fold_in(own_key, 1), shape, 0, int(table[len(portions) - 1]))
    start = jnp.left_shift(1, jnp.searchsorted(jnp.asarray(table, jnp.int32), pick, side="right").astype(jnp.int32))
    rank = start - 1 + jax.random.randint(jax.random.fold_in(own_key, 4), shape, 0, 1 << 30) % jnp.minimum(start, count + 1 - start)
    return jax.random.permutation(jax.random.fold_in(own_key, 2), count)[rank].astype(jnp.int32)


def setup_inputs(seed: int = 0) -> dict:
    key_list = jax.random.split(jax.random.key(seed), 7)
    return {
        "teacher_logits": draw_teacher_logits(jax.random.fold_in(key_list[6], 71), 0),
        "hidden": draw_hidden(jax.random.fold_in(key_list[6], 71), 0),
        "new_head": draw_new_head(jax.random.fold_in(key_list[6], 71), 0),
        "labels": with_ends(ranked_wide(key_list[3], (TOKENS,), V_NEW, 2), jax.random.fold_in(key_list[3], 3), 0, V_NEW - 1).astype(jnp.int32),
        "map_target": draw_map_target(jax.random.fold_in(key_list[6], 71), 0),
        "map_weight": draw_map_weight(jax.random.fold_in(key_list[6], 71), 0),
    }


def reference(teacher_logits, hidden, new_head, labels, map_target, map_weight):
    scores = teacher_logits.astype(jnp.float32)
    highest = jnp.max(scores, axis=1, keepdims=True)
    raised = jnp.exp(scores - highest)
    teacher_prob = (raised / jnp.sum(raised, axis=1, keepdims=True)).astype(jnp.bfloat16)
    blocks = teacher_prob.reshape(TOKENS, OB_ALL, BLK).astype(jnp.float32)
    target = jnp.zeros((TOKENS, NEW_BLOCKS, BLK), jnp.float32)
    for column in range(FAN):
        mapped = jnp.einsum('tjb,jbc->tjc', blocks, map_weight[:, column].astype(jnp.float32))
        mapped = lax.optimization_barrier(mapped.astype(jnp.bfloat16)).astype(jnp.float32)
        target = target.at[:, map_target[:, column], :].add(mapped)
    target = target.reshape(TOKENS, V_NEW)
    logits = jnp.dot(hidden, new_head, preferred_element_type=jnp.float32)
    row_top = jnp.max(logits, axis=1)
    log_total = row_top + jnp.log(jnp.sum(jnp.exp(logits - row_top[:, None]), axis=1))
    target_mass = jnp.sum(target, axis=1)
    inner = jnp.sum(target * logits, axis=1)
    label_hit = jnp.arange(V_NEW, dtype=jnp.int32)[None, :] == labels[:, None]
    label_logit = jnp.sum(jnp.where(label_hit, logits, 0.0), axis=1)
    loss = target_mass * log_total - inner + log_total - label_logit
    probs = jnp.exp(logits - log_total[:, None])
    grad_logits = ((target_mass + 1.0)[:, None] * probs - target - label_hit.astype(jnp.float32)).astype(jnp.bfloat16)
    head_grad = lax.dot_general(hidden, grad_logits, (((0,), (0,)), ((), ())), preferred_element_type=jnp.float32)
    return loss, head_grad.astype(jnp.bfloat16)
```

```python
import functools

import jax
import jax.numpy as jnp
from jax import lax
from jax.experimental import pallas as pl
from jax.experimental.pallas import tpu as pltpu
from jax.sharding import PartitionSpec as P

MESH = pl.DeviceIdType.MESH
F32 = jnp.float32
BF16 = jnp.bfloat16

NY = 4
NX = 4
NZ = 4
NC = 2
ROWS = 128
HALF = 64
BLK = 128
FAN = 4
D = 4608
HD = D // 2
VN = 1024
PER = 8
OLD = 32
ENT = OLD * FAN

FIRST = [(0, 1), (1, 0), (1, 1), (2, 0), (2, 1), (3, 0), (3, 1)]


def vocab_index(x, z, c):
    return (x * NZ + z) * NC + c


def as_row(column):
    return jnp.transpose(jnp.broadcast_to(column, (ROWS, BLK)))[0:1, :]


def as_column(row):
    return jnp.transpose(jnp.broadcast_to(row, (ROWS, BLK)))


def exchange_kernel(
    entry_ref, valid_ref, mask_ref, label_ref, raw_hbm, hidden_hbm, head_hbm, weight_hbm,
    loss_ref, grad_ref, everyone_hbm,
    raw, prob, weight, hidden, head, logits, out1, in1, out2, in2, masks, mass_acc,
    log_total, mass_plus, rest,
    t1_out, t1_in, t2_out, t2_in, t3_out, t3_in,
    a1_out, a1_in, a2_out, a2_in, a3_out, a3_in,
    f1_out, f1_in, f2_out, f2_in, f3_out, f3_in,
    local_sem, raw_send, raw_recv, mask_send, mask_recv, p1_send, p1_recv, p2_send, p2_recv,
    hid_send, hid_recv, sib_send, sib_recv,
    t1_send, t1_recv, t2_send, t2_recv, t3_send, t3_recv,
    a1_send, a1_recv, a2_send, a2_recv, a3_send, a3_recv,
    f1_send, f1_recv, f2_send, f2_recv, f3_send, f3_recv,
):
    y = lax.axis_index("tok")
    v = lax.axis_index("vocab")
    x = v // (NZ * NC)
    z = (v // NC) % NZ
    c = v % NC

    def remote(src, dst, send, recv, device):
        return pltpu.make_async_remote_copy(
            src_ref=src, dst_ref=dst, send_sem=send, recv_sem=recv,
            device_id=device, device_id_type=MESH,
        )

    def along_x(step, core_step=0):
        return (y, vocab_index((x + step) % NX, z, (c + core_step) % NC))

    def along_z(step, core_step=0):
        return (y, vocab_index(x, (z + step) % NZ, (c + core_step) % NC))

    def along_y(step):
        return ((y + step) % NY, v)

    load_raw = pltpu.make_async_copy(raw_hbm, raw.at[0], local_sem.at[0])
    load_weight = pltpu.make_async_copy(weight_hbm, weight, local_sem.at[1])
    own_rows = pl.ds(pl.multiple_of(y * ROWS, ROWS), ROWS)
    load_hidden = pltpu.make_async_copy(hidden_hbm, hidden.at[own_rows], local_sem.at[2])
    load_head = pltpu.make_async_copy(head_hbm, head, local_sem.at[3])
    load_raw.start()
    load_weight.start()
    load_hidden.start()
    load_head.start()

    barrier = pltpu.get_barrier_semaphore()
    partners = [along_x(da, dc) for da, dc in FIRST]
    partners += [along_z(da, dc) for da, dc in FIRST if da]
    partners += [along_y(step) for step in (1, 2, 3)]
    for partner in partners:
        pl.semaphore_signal(barrier, inc=1, device_id=partner, device_id_type=MESH)
    pl.semaphore_wait(barrier, len(partners))

    def first_partner(h, i):
        da, dc = FIRST[i]
        return along_x(da, dc) if h == 0 else along_z(da, dc)

    def mask_copy(h, i):
        da, dc = FIRST[i]
        c2 = (c + dc) % NC
        if h == 0:
            src = mask_ref.at[(x + da) % NX, :, c2]
        else:
            src = mask_ref.at[:, (z + da) % NZ, c2]
        return remote(src, masks.at[h, i], mask_send.at[h, i], mask_recv.at[h, i],
                      first_partner(h, i))

    def first_copy(g, h, i):
        da, dc = FIRST[i]
        c2 = (c + dc) % NC
        rows = pl.ds(h * HALF, HALF)
        if h == 0:
            src = out1.at[g, (x + da) % NX, :, c2, :, rows]
        else:
            src = out1.at[g, :, (z + da) % NZ, c2, :, rows]
        return remote(src, in1.at[g, h, i], p1_send.at[g, h, i], p1_recv.at[g, h, i],
                      first_partner(h, i))

    def second_copy(g, h, d):
        if h == 0:
            q, device = (z + d) % NZ, along_z(d)
        else:
            q, device = (x + d) % NX, along_x(d)
        return remote(out2.at[g, h, q], in2.at[g, h, d - 1], p2_send.at[g, h, d - 1],
                      p2_recv.at[g, h, d - 1], device)

    upper, lower = pl.ds(0, HALF), pl.ds(HALF, HALF)
    raw_copies = [
        remote(raw.at[0], raw.at[1], raw_send.at[0], raw_recv.at[0], along_y(1)),
        remote(raw.at[0], raw.at[3], raw_send.at[1], raw_recv.at[1], along_y(3)),
        remote(raw.at[1, upper], raw.at[2, upper], raw_send.at[2], raw_recv.at[2], along_y(1)),
        remote(raw.at[3, lower], raw.at[2, lower], raw_send.at[3], raw_recv.at[3], along_y(3)),
    ]

    own_columns = pl.ds(pl.multiple_of(c * HD, HD), HD)

    def rows_of(d):
        return pl.ds(pl.multiple_of(((y - d + NY) % NY) * ROWS, ROWS), ROWS)

    def hidden_copy(d):
        part = hidden.at[own_rows, own_columns]
        return remote(part, part, hid_send.at[d - 1], hid_recv.at[d - 1], along_y(d))

    def sibling_copy(d):
        part = hidden.at[rows_of(d), own_columns]
        return remote(part, part, sib_send.at[d - 1], sib_recv.at[d - 1], along_x(0, 1))

    def stage_x(out, into, send, recv):
        return [remote(out, into.at[i], send.at[i], recv.at[i], first_partner(0, i))
                for i in range(7)]

    def stage_z(out, into, send, recv):
        return [remote(out, into.at[d - 1], send.at[d - 1], recv.at[d - 1], along_z(d))
                for d in (1, 2, 3)]

    def stage_y(out, into, send, recv):
        return [remote(out, into.at[d - 1], send.at[d - 1], recv.at[d - 1], along_y(d))
                for d in (1, 2, 3)]

    pending = []

    def start(copies):
        for copy in copies:
            copy.start()
        pending.extend(copies)

    def arrived(copies):
        for copy in copies:
            copy.wait_recv()

    load_raw.wait()
    start(raw_copies[:2])
    mask_copies = [mask_copy(h, i) for h in (0, 1) for i in range(7)]
    start(mask_copies)

    def block_max(j, acc):
        part = raw[0, :, pl.ds(pl.multiple_of(j * BLK, BLK), BLK)].astype(F32)
        return jnp.maximum(acc, part)

    top = lax.fori_loop(1, OLD, block_max, raw[0, :, pl.ds(0, BLK)].astype(F32), unroll=4)
    top = jnp.broadcast_to(jnp.max(top, axis=1, keepdims=True), (ROWS, BLK))

    def block_sum(j, acc):
        part = raw[0, :, pl.ds(pl.multiple_of(j * BLK, BLK), BLK)].astype(F32)
        return acc + jnp.exp(part - top)

    total = lax.fori_loop(0, OLD, block_sum, jnp.zeros((ROWS, BLK), F32), unroll=4)
    total = jnp.sum(total, axis=1, keepdims=True)
    sublane = lax.broadcasted_iota(jnp.int32, (8, BLK), 0)

    def stacked(first, second):
        return jnp.where(sublane == 0, jnp.broadcast_to(first, (8, BLK)),
                         jnp.broadcast_to(second, (8, BLK)))

    def joined(pairs):
        best = functools.reduce(jnp.maximum, [p[0:1] for p in pairs])
        mass = functools.reduce(jnp.add, [p[1:2] * jnp.exp(p[0:1] - best) for p in pairs])
        return stacked(best, mass)

    t1_out[...] = stacked(as_row(top[:, 0:1]), as_row(total))
    copies = stage_x(t1_out, t1_in, t1_send, t1_recv)
    start(copies)
    arrived(copies)
    t2_out[...] = joined([t1_out[...]] + [t1_in[i] for i in range(7)])
    copies = stage_z(t2_out, t2_in, t2_send, t2_recv)
    start(copies)
    arrived(copies)
    t3_out[...] = joined([t2_out[...]] + [t2_in[i] for i in range(3)])
    t3_copies = stage_y(t3_out, t3_in, t3_send, t3_recv)
    start(t3_copies)
    load_weight.wait()

    def contribute(g):
        stats = t3_out[...] if g == 0 else t3_in[g - 1]
        best = as_column(stats[0:1])
        inverse = as_column(1.0 / stats[1:2])

        def normalise(j, carry):
            part = raw[g, :, pl.ds(pl.multiple_of(j * BLK, BLK), BLK)].astype(F32)
            prob[j] = (jnp.exp(part - best) * inverse).astype(BF16)
            return carry

        lax.fori_loop(0, OLD, normalise, 0, unroll=2)

        def slot(o, acc):
            for k in range(2):
                e = entry_ref[o * 2 + k]
                product = jnp.dot(prob[e // FAN], weight[e], preferred_element_type=F32)
                product = product.astype(BF16)
                out1[g, o // (NZ * NC), (o // NC) % NZ, o % NC, k] = product
                acc = acc + product.astype(F32) * valid_ref[o * 2 + k]
            return acc

        acc = lax.fori_loop(0, 32, slot, jnp.zeros((ROWS, BLK), F32), unroll=2)
        mass_acc[g] = acc
        start([first_copy(g, h, i) for i in range(7) for h in (0, 1)])

    def merge(g, h):
        arrived([first_copy(g, h, i) for i in range(7)])

        def piece(t, carry):
            q, rows = t // 2, pl.ds(pl.multiple_of((t % 2) * 32, 32), 32)
            own = pl.ds(pl.multiple_of(h * HALF + (t % 2) * 32, 32), 32)
            sums = [jnp.zeros((32, BLK), F32) for _ in range(PER)]
            for i in range(8):
                for k in range(2):
                    if i < 7:
                        part, hit = in1[g, h, i, q, k, rows], masks[h, i, q, k]
                    elif h == 0:
                        part, hit = out1[g, x, q, c, k, own], mask_ref[x, q, c, k]
                    else:
                        part, hit = out1[g, q, z, c, k, own], mask_ref[q, z, c, k]
                    part = part.astype(F32)
                    for b in range(PER):
                        sums[b] = sums[b] + part * hit[b : b + 1]
            for b in range(PER):
                out2[g, h, q, b, rows] = sums[b].astype(BF16)
            return carry

        lax.fori_loop(0, 8, piece, 0)
        start([second_copy(g, h, d) for d in (1, 2, 3)])

    contribute(0)
    arrived([raw_copies[0]])
    start([raw_copies[2]])
    arrived([raw_copies[1]])
    start([raw_copies[3]])
    arrived(t3_copies)
    contribute(1)
    load_hidden.wait()
    contribute(3)
    arrived(mask_copies)
    hidden_copies = [hidden_copy(d) for d in (1, 2, 3)]
    merge(0, 0)
    merge(0, 1)
    arrived(raw_copies[2:])
    start(hidden_copies)
    contribute(2)
    merge(1, 0)
    merge(1, 1)
    merge(3, 0)
    merge(3, 1)
    arrived(hidden_copies)
    sibling_copies = [sibling_copy(d) for d in (1, 2, 3)]
    start(sibling_copies)
    merge(2, 0)
    merge(2, 1)
    arrived(sibling_copies)
    keep = pltpu.make_async_copy(hidden, everyone_hbm, local_sem.at[4])
    keep.start()
    load_head.wait()

    def columns_of(n, carry):
        columns = pl.ds(pl.multiple_of(n * 256, 256), 256)
        logits[:, columns] = jnp.dot(hidden[...], head[:, columns], preferred_element_type=F32)
        return carry

    lax.fori_loop(0, VN // 256, columns_of, 0)

    sublane3 = lax.broadcasted_iota(jnp.int32, (8, BLK), 0)

    def triple(first, second, third):
        wide = [jnp.broadcast_to(r, (8, BLK)) for r in (first, second, third)]
        return jnp.where(sublane3 == 0, wide[0], jnp.where(sublane3 == 1, wide[1], wide[2]))

    for g in range(NY):
        group = (y - g + NY) % NY
        rows = pl.ds(pl.multiple_of(group * ROWS, ROWS), ROWS)
        best = logits[rows, pl.ds(0, BLK)]
        for b in range(1, PER):
            best = jnp.maximum(best, logits[rows, pl.ds(b * BLK, BLK)])
        best = jnp.broadcast_to(jnp.max(best, axis=1, keepdims=True), (ROWS, BLK))
        acc = jnp.zeros((ROWS, BLK), F32)
        for b in range(PER):
            acc = acc + jnp.exp(logits[rows, pl.ds(b * BLK, BLK)] - best)
        a1_out[group] = triple(
            as_row(best[:, 0:1]),
            as_row(jnp.sum(acc, axis=1, keepdims=True)),
            as_row(jnp.sum(mass_acc[g], axis=1, keepdims=True)),
        )

    def joined3(parts):
        best = functools.reduce(jnp.maximum, [p[0:1] for p in parts])
        exps = functools.reduce(jnp.add, [p[1:2] * jnp.exp(p[0:1] - best) for p in parts])
        mass = functools.reduce(jnp.add, [p[2:3] for p in parts])
        return triple(best, exps, mass)

    def combine(out, own, into, count):
        for q in range(NY):
            out[q] = joined3([own[q]] + [into[i, q] for i in range(count)])

    copies = stage_x(a1_out, a1_in, a1_send, a1_recv)
    start(copies)
    arrived(copies)
    combine(a2_out, a1_out, a1_in, 7)
    copies = stage_z(a2_out, a2_in, a2_send, a2_recv)
    start(copies)
    arrived(copies)
    combine(a3_out, a2_out, a2_in, 3)
    copies = stage_y(a3_out, a3_in, a3_send, a3_recv)
    start(copies)
    arrived(copies)
    for q in range(NY):
        stats = joined3([a3_out[q]] + [a3_in[i, q] for i in range(3)])
        rows = pl.ds(q * ROWS, ROWS)
        log_total[rows] = as_column(stats[0:1] + jnp.log(stats[1:2]))
        mass_plus[rows] = as_column(stats[2:3] + 1.0)
        f1_out[q] = stats

    mine = f1_out[y]
    own_log = mine[0:1] + jnp.log(mine[1:2])
    own_terms = mine[2:3] * own_log + own_log

    base = (y * (NX * NZ * NC) + v) * VN
    lane = lax.broadcasted_iota(jnp.int32, (32, BLK), 1) + base

    def finish(g, h):
        arrived([second_copy(g, h, d) for d in (1, 2, 3)])
        group = (y - g + NY) % NY
        q = z if h == 0 else x

        def piece(t, carry):
            part = pl.ds(pl.multiple_of(t * 32, 32), 32)
            rows = pl.ds(pl.multiple_of(group * ROWS + h * HALF + t * 32, 32), 32)
            log_here, mass_here, label_here = log_total[rows], mass_plus[rows], label_ref[rows]
            acc = jnp.zeros((32, BLK), F32)
            for b in range(PER):
                target = out2[g, h, q, b, part].astype(F32)
                for d in range(3):
                    target = target + in2[g, h, d, b, part].astype(F32)
                columns = pl.ds(b * BLK, BLK)
                here = logits[rows, columns]
                hit = (label_here == lane + b * BLK).astype(F32)
                acc = acc + (target + hit) * here
                grad = mass_here * jnp.exp(here - log_here) - target - hit
                grad_ref[rows, columns] = grad.astype(BF16)
            rest[rows] = acc
            return carry

        lax.fori_loop(0, HALF // 32, piece, 0)

    for g in (0, 1, 3, 2):
        for h in (0, 1):
            finish(g, h)

    for q in range(NY):
        column = jnp.sum(rest[pl.ds(q * ROWS, ROWS)], axis=1, keepdims=True)
        f1_out[q] = jnp.broadcast_to(as_row(column), (8, BLK))
    copies = [remote(f1_out.at[(y + d) % NY], f1_in.at[d - 1], f1_send.at[d - 1],
                     f1_recv.at[d - 1], along_y(d)) for d in (1, 2, 3)]
    start(copies)
    arrived(copies)
    f2_out[...] = f1_out[y] + (f1_in[0] + f1_in[1] + f1_in[2])
    copies = stage_x(f2_out, f2_in, f2_send, f2_recv)
    start(copies)
    arrived(copies)
    f3_out[...] = functools.reduce(jnp.add, [f2_out[...]] + [f2_in[i] for i in range(7)])
    copies = stage_z(f3_out, f3_in, f3_send, f3_recv)
    start(copies)
    arrived(copies)
    everything = f3_out[...] + (f3_in[0] + f3_in[1] + f3_in[2])
    loss_ref[...] = own_terms - everything[0:1]

    keep.wait()
    for copy in pending:
        copy.wait_send()


def exchange(entry, valid, mask, label, raw, hidden, head, weight):
    dma = pltpu.SemaphoreType.DMA
    vmem = pltpu.VMEM
    tile, quad = (8, BLK), (NY, 8, BLK)
    scratch = [
        vmem((NY, ROWS, OLD * BLK), BF16),
        vmem((OLD, ROWS, BLK), BF16),
        vmem((ENT, BLK, BLK), BF16),
        vmem((NY * ROWS, D), BF16),
        vmem((D, VN), BF16),
        vmem((NY * ROWS, VN), F32),
        vmem((NY, NX, NZ, NC, 2, ROWS, BLK), BF16),
        vmem((NY, 2, 7, 4, 2, HALF, BLK), BF16),
        vmem((NY, 2, 4, PER, HALF, BLK), BF16),
        vmem((NY, 2, 3, PER, HALF, BLK), BF16),
        vmem((2, 7, 4, 2, 8, BLK), F32),
        vmem((NY, ROWS, BLK), F32),
        vmem((NY * ROWS, BLK), F32),
        vmem((NY * ROWS, BLK), F32),
        vmem((NY * ROWS, BLK), F32),
        vmem(tile, F32), vmem((7,) + tile, F32),
        vmem(tile, F32), vmem((3,) + tile, F32),
        vmem(tile, F32), vmem((3,) + tile, F32),
        vmem(quad, F32), vmem((7,) + quad, F32),
        vmem(quad, F32), vmem((3,) + quad, F32),
        vmem(quad, F32), vmem((3,) + quad, F32),
        vmem(quad, F32), vmem((3,) + tile, F32),
        vmem(tile, F32), vmem((7,) + tile, F32),
        vmem(tile, F32), vmem((3,) + tile, F32),
        dma((5,)), dma((4,)), dma((4,)), dma((2, 7)), dma((2, 7)),
        dma((NY, 2, 7)), dma((NY, 2, 7)), dma((NY, 2, 3)), dma((NY, 2, 3)),
        dma((3,)), dma((3,)), dma((3,)), dma((3,)),
    ]
    for count in (7, 3, 3, 7, 3, 3, 3, 7, 3):
        scratch += [dma((count,)), dma((count,))]
    smem = pl.BlockSpec(memory_space=pltpu.SMEM)
    inside = pl.BlockSpec(memory_space=pltpu.VMEM)
    outside = pl.BlockSpec(memory_space=pl.ANY)
    return pl.pallas_call(
        exchange_kernel,
        out_shape=(
            jax.ShapeDtypeStruct((1, ROWS), F32),
            jax.ShapeDtypeStruct((NY * ROWS, VN), BF16),
            jax.ShapeDtypeStruct((NY * ROWS, D), BF16),
        ),
        in_specs=[smem, smem, inside, inside] + [outside] * 4,
        out_specs=(inside, inside, outside),
        scratch_shapes=scratch,
        compiler_params=pltpu.CompilerParams(
            collective_id=0, has_side_effects=True, vmem_limit_bytes=60 << 20
        ),
        name="exchange",
    )(entry, valid, mask, label, raw, hidden, head, weight)


GRAD_ROWS = 512


def grad_kernel(hidden_ref, grad_ref, out_ref):
    out_ref[...] = lax.dot_general(
        hidden_ref[...], grad_ref[...], (((0,), (0,)), ((), ())), preferred_element_type=F32
    ).astype(BF16)


def head_gradient(hidden, grad):
    return pl.pallas_call(
        grad_kernel,
        grid=(D // GRAD_ROWS,),
        out_shape=jax.ShapeDtypeStruct((D, VN), BF16),
        in_specs=[
            pl.BlockSpec((NY * ROWS, GRAD_ROWS), lambda i: (0, i)),
            pl.BlockSpec((NY * ROWS, VN), lambda i: (0, 0)),
        ],
        out_specs=pl.BlockSpec((GRAD_ROWS, VN), lambda i: (i, 0)),
        compiler_params=pltpu.CompilerParams(vmem_limit_bytes=32 << 20),
        name="head_gradient",
    )(hidden, grad)


def local(teacher_logits, hidden, new_head, labels, map_target, map_weight):
    y = lax.axis_index("tok")
    nodes = NX * NZ * NC
    flat = map_target.reshape(1, ENT)
    owner = flat // PER - y * nodes
    match = owner == jnp.arange(nodes, dtype=jnp.int32)[:, None]
    index = jnp.arange(ENT, dtype=jnp.int32)[None, :]
    key = index * PER + flat % PER
    none = ENT * PER
    first = jnp.min(jnp.where(match, key, none), axis=1)
    last = jnp.max(jnp.where(match, key, -1), axis=1)
    keys = jnp.stack([first, last], axis=1)
    valid = jnp.stack([first < none, last > first], axis=1)
    keys = jnp.where(valid, keys, 0)
    entry = (keys // PER).reshape(2 * nodes)
    block = (keys % PER)[:, :, None]
    mask = (block == jnp.arange(PER)[None, None, :]) & valid[:, :, None]
    mask = jnp.broadcast_to(mask.astype(F32)[..., None], (nodes, 2, PER, BLK))
    mask = mask.reshape(NX, NZ, NC, 2, PER, BLK)
    label = jnp.broadcast_to(labels[:, None], (NY * ROWS, BLK))
    loss, grad, everyone = exchange(
        entry, valid.astype(F32).reshape(2 * nodes), mask, label,
        teacher_logits, hidden, new_head, map_weight.reshape(ENT, BLK, BLK),
    )
    return loss.reshape(ROWS), head_gradient(everyone, grad)


def solution(mesh):
    return jax.shard_map(
        local,
        mesh=mesh,
        in_specs=(
            P("tok", "vocab"),
            P("tok", None),
            P(None, ("tok", "vocab")),
            P(),
            P("vocab", None),
            P("vocab", None, None, None),
        ),
        out_specs=(P("tok"), P(None, ("tok", "vocab"))),
        check_vma=False,
    )
```

```python
import functools

import jax
import jax.numpy as jnp
from jax import lax
from jax.experimental import pallas as pl
from jax.experimental.pallas import tpu as pltpu
from jax.sharding import PartitionSpec as P

MESH = pl.DeviceIdType.MESH
F32 = jnp.float32
BF16 = jnp.bfloat16

NY = 4
NX = 4
NZ = 4
NC = 2
ROWS = 128
CHUNK = 64
HALF = CHUNK // 2
NU = NY * ROWS // CHUNK
BLK = 128
FAN = 4
D = 4608
HD = D // 2
VN = 1024
PER = 8
OLD = 32
ENT = OLD * FAN

FIRST = [(0, 1), (1, 0), (1, 1), (2, 0), (2, 1), (3, 0), (3, 1)]


def vocab_index(x, z, c):
    return (x * NZ + z) * NC + c


def as_row(column):
    return jnp.transpose(jnp.broadcast_to(column, (ROWS, BLK)))[0:1, :]


def as_column(row):
    return jnp.transpose(jnp.broadcast_to(row, (ROWS, BLK)))


def exchange_kernel(
    key_ref, label_ref, raw_hbm, hidden_hbm, head_hbm, weight_hbm,
    loss_ref, grad_ref, everyone_hbm,
    mask_ref, raw, prob, weight, hidden, head, logits, target, out1, in1, out2, in2, masks, mass_acc,
    log_total, mass_plus, label_at, rest,
    t1_out, t1_in, t2_out, t2_in, t3_out, t3_in,
    a1_out, a1_in, a2_out, a2_in, a3_out, a3_in,
    f1_out, f1_in, f2_out, f2_in, f3_out, f3_in,
    local_sem, raw_send, raw_recv, mask_send, mask_recv, p1_send, p1_recv, p2_send, p2_recv,
    hid_send, hid_recv, sib_send, sib_recv,
    t1_send, t1_recv, t2_send, t2_recv, t3_send, t3_recv,
    a1_send, a1_recv, a2_send, a2_recv, a3_send, a3_recv,
    f1_send, f1_recv, f2_send, f2_recv, f3_send, f3_recv,
):
    y = lax.axis_index("tok")
    v = lax.axis_index("vocab")
    x = v // (NZ * NC)
    z = (v // NC) % NZ
    c = v % NC

    def remote(src, dst, send, recv, device):
        return pltpu.make_async_remote_copy(
            src_ref=src, dst_ref=dst, send_sem=send, recv_sem=recv,
            device_id=device, device_id_type=MESH,
        )

    def along_x(step, core_step=0):
        return (y, vocab_index((x + step) % NX, z, (c + core_step) % NC))

    def along_z(step, core_step=0):
        return (y, vocab_index(x, (z + step) % NZ, (c + core_step) % NC))

    def along_y(step):
        return ((y + step) % NY, v)

    load_raw = pltpu.make_async_copy(raw_hbm, raw.at[0], local_sem.at[0])
    load_weight = pltpu.make_async_copy(weight_hbm, weight, local_sem.at[1])
    own_rows = pl.ds(pl.multiple_of(y * ROWS, ROWS), ROWS)
    load_hidden = pltpu.make_async_copy(hidden_hbm, hidden.at[own_rows], local_sem.at[2])
    load_head = pltpu.make_async_copy(head_hbm, head, local_sem.at[3])
    load_raw.start()

    barrier = pltpu.get_barrier_semaphore()
    partners = [along_x(da, dc) for da, dc in FIRST]
    partners += [along_z(da, dc) for da, dc in FIRST if da]
    partners += [along_y(step) for step in (1, 2, 3)]
    for partner in partners:
        pl.semaphore_signal(barrier, inc=1, device_id=partner, device_id_type=MESH)
    pl.semaphore_wait(barrier, len(partners))

    def first_partner(h, i):
        da, dc = FIRST[i]
        return along_x(da, dc) if h == 0 else along_z(da, dc)

    def mask_copy(h, i):
        da, dc = FIRST[i]
        c2 = (c + dc) % NC
        if h == 0:
            src = mask_ref.at[(x + da) % NX, :, c2]
        else:
            src = mask_ref.at[:, (z + da) % NZ, c2]
        return remote(src, masks.at[h, i], mask_send.at[h, i], mask_recv.at[h, i],
                      first_partner(h, i))

    def first_copy(u, h, i):
        da, dc = FIRST[i]
        c2 = (c + dc) % NC
        rows = pl.ds(h * HALF, HALF)
        if h == 0:
            src = out1.at[u, (x + da) % NX, :, c2, :, rows]
        else:
            src = out1.at[u, :, (z + da) % NZ, c2, :, rows]
        return remote(src, in1.at[u, h, i], p1_send.at[u, h, i], p1_recv.at[u, h, i],
                      first_partner(h, i))

    def second_copy(u, h, d):
        if h == 0:
            q, device = (z + d) % NZ, along_z(d)
        else:
            q, device = (x + d) % NX, along_x(d)
        return remote(out2.at[u, h, q], in2.at[u, h, d - 1], p2_send.at[u, h, d - 1],
                      p2_recv.at[u, h, d - 1], device)

    upper, lower = pl.ds(0, CHUNK), pl.ds(CHUNK, CHUNK)
    raw_copies = [
        remote(raw.at[source, rows], raw.at[into, rows], raw_send.at[i], raw_recv.at[i], along_y(d))
        for i, (source, into, rows, d) in enumerate([
            (0, 1, upper, 1), (0, 3, lower, 3), (0, 1, lower, 1), (0, 3, upper, 3),
            (1, 2, upper, 1), (3, 2, lower, 3),
        ])
    ]

    own_columns = pl.ds(pl.multiple_of(c * HD, HD), HD)

    def hidden_part(d, first=0, count=ROWS):
        start_row = ((y - d + NY) % NY) * ROWS + first
        rows = pl.ds(pl.multiple_of(start_row, CHUNK), count)
        return hidden.at[rows, own_columns]

    hidden_copies = [
        remote(hidden_part(*what), hidden_part(*what), hid_send.at[i], hid_recv.at[i], along_y(d))
        for i, (what, d) in enumerate([
            ((0, 0, CHUNK), 1), ((0, CHUNK, CHUNK), 3), ((0, CHUNK, CHUNK), 1), ((0, 0, CHUNK), 3),
            ((1, 0, CHUNK), 1), ((3, CHUNK, CHUNK), 3),
        ])
    ]

    def sibling_copy(d):
        part = hidden_part(d)
        return remote(part, part, sib_send.at[d - 1], sib_recv.at[d - 1], along_x(0, 1))

    def stage_x(out, into, send, recv):
        return [remote(out, into.at[i], send.at[i], recv.at[i], first_partner(0, i))
                for i in range(7)]

    def stage_z(out, into, send, recv):
        return [remote(out, into.at[d - 1], send.at[d - 1], recv.at[d - 1], along_z(d))
                for d in (1, 2, 3)]

    def stage_y(out, into, send, recv):
        return [remote(out, into.at[d - 1], send.at[d - 1], recv.at[d - 1], along_y(d))
                for d in (1, 2, 3)]

    pending = []

    def start(copies):
        for copy in copies:
            copy.start()
        pending.extend(copies)

    def arrived(copies):
        for copy in copies:
            copy.wait_recv()

    sublane = lax.broadcasted_iota(jnp.int32, (8, BLK), 0)

    def mask_rows(o, carry):
        for k in range(2):
            key = key_ref[o * 2 + k]
            row = jnp.where(key < 0, -1, key % PER)
            mask_ref[o // (NZ * NC), (o // NC) % NZ, o % NC, k] = (sublane == row).astype(F32)
        return carry

    lax.fori_loop(0, NX * NZ * NC, mask_rows, 0, unroll=4)
    load_raw.wait()
    start(raw_copies[:2])
    load_weight.start()
    load_hidden.start()
    load_head.start()
    mask_copies = [mask_copy(h, i) for h in (0, 1) for i in range(7)]
    start(mask_copies)

    def block_max(j, acc):
        part = raw[0, :, pl.ds(pl.multiple_of(j * BLK, BLK), BLK)].astype(F32)
        return jnp.maximum(acc, part)

    top = lax.fori_loop(1, OLD, block_max, raw[0, :, pl.ds(0, BLK)].astype(F32), unroll=4)
    top = jnp.broadcast_to(jnp.max(top, axis=1, keepdims=True), (ROWS, BLK))

    def block_sum(j, acc):
        part = raw[0, :, pl.ds(pl.multiple_of(j * BLK, BLK), BLK)].astype(F32)
        return acc + jnp.exp(part - top)

    total = lax.fori_loop(0, OLD, block_sum, jnp.zeros((ROWS, BLK), F32), unroll=4)
    total = jnp.sum(total, axis=1, keepdims=True)
    def stacked(first, second):
        return jnp.where(sublane == 0, jnp.broadcast_to(first, (8, BLK)),
                         jnp.broadcast_to(second, (8, BLK)))

    def joined(pairs):
        best = functools.reduce(jnp.maximum, [p[0:1] for p in pairs])
        mass = functools.reduce(jnp.add, [p[1:2] * jnp.exp(p[0:1] - best) for p in pairs])
        return stacked(best, mass)

    t1_out[...] = stacked(as_row(top[:, 0:1]), as_row(total))
    copies = stage_x(t1_out, t1_in, t1_send, t1_recv)
    start(copies)
    arrived(copies)
    t2_out[...] = joined([t1_out[...]] + [t1_in[i] for i in range(7)])
    copies = stage_z(t2_out, t2_in, t2_send, t2_recv)
    start(copies)
    arrived(copies)
    t3_out[...] = joined([t2_out[...]] + [t2_in[i] for i in range(3)])
    t3_copies = stage_y(t3_out, t3_in, t3_send, t3_recv)
    start(t3_copies)
    load_weight.wait()

    def contribute(g, part):
        u = g * 2 + part
        tokens = pl.ds(part * CHUNK, CHUNK)
        stats = t3_out[...] if g == 0 else t3_in[g - 1]
        best = as_column(stats[0:1])[part * CHUNK : (part + 1) * CHUNK]
        inverse = as_column(1.0 / stats[1:2])[part * CHUNK : (part + 1) * CHUNK]

        def normalise(j, carry):
            scores = raw[g, tokens, pl.ds(pl.multiple_of(j * BLK, BLK), BLK)].astype(F32)
            prob[j] = (jnp.exp(scores - best) * inverse).astype(BF16)
            return carry

        lax.fori_loop(0, OLD, normalise, 0, unroll=4)

        def slot(o, acc):
            for k in range(2):
                key = key_ref[o * 2 + k]
                e = jnp.maximum(key, 0) // PER
                filled = jnp.where(key < 0, 0.0, 1.0)
                product = jnp.dot(prob[e // FAN], weight[e], preferred_element_type=F32)
                product = product.astype(BF16)
                out1[u, o // (NZ * NC), (o // NC) % NZ, o % NC, k] = product
                acc = acc + product.astype(F32) * filled
            return acc

        acc = lax.fori_loop(0, 32, slot, jnp.zeros((CHUNK, BLK), F32), unroll=4)
        mass_acc[g, tokens] = acc
        start([first_copy(u, h, i) for i in range(7) for h in (0, 1)])

    def merge(u, h):
        arrived([first_copy(u, h, i) for i in range(7)])
        own = pl.ds(h * HALF, HALF)

        def piece(q, carry):
            sums = [jnp.zeros((HALF, BLK), F32) for _ in range(PER)]
            for i in range(8):
                for k in range(2):
                    if i < 7:
                        part, hit = in1[u, h, i, q, k], masks[h, i, q, k]
                    elif h == 0:
                        part, hit = out1[u, x, q, c, k, own], mask_ref[x, q, c, k]
                    else:
                        part, hit = out1[u, q, z, c, k, own], mask_ref[q, z, c, k]
                    part = part.astype(F32)
                    for b in range(PER):
                        sums[b] = sums[b] + part * hit[b : b + 1]
            for b in range(PER):
                out2[u, h, q, b] = sums[b].astype(BF16)
            return carry

        lax.fori_loop(0, 4, piece, 0)
        start([second_copy(u, h, d) for d in (1, 2, 3)])

    def merge_all(*units):
        for u in units:
            for h in (0, 1):
                merge(u, h)

    def group_rows(g, first=0, count=ROWS):
        start_row = ((y - g + NY) % NY) * ROWS + first
        return pl.ds(pl.multiple_of(start_row, HALF), count)

    def student(g):
        rows = group_rows(g)

        def columns_of(n, carry):
            columns = pl.ds(pl.multiple_of(n * 256, 256), 256)
            logits[rows, columns] = jnp.dot(
                hidden[rows, :], head[:, columns], preferred_element_type=F32
            )
            return carry

        lax.fori_loop(0, VN // 256, columns_of, 0)
        best = logits[rows, pl.ds(0, BLK)]
        for b in range(1, PER):
            best = jnp.maximum(best, logits[rows, pl.ds(b * BLK, BLK)])
        best = jnp.broadcast_to(jnp.max(best, axis=1, keepdims=True), (ROWS, BLK))
        acc = jnp.zeros((ROWS, BLK), F32)
        for b in range(PER):
            acc = acc + jnp.exp(logits[rows, pl.ds(b * BLK, BLK)] - best)
        a1_out[(y - g + NY) % NY] = triple(
            as_row(best[:, 0:1]),
            as_row(jnp.sum(acc, axis=1, keepdims=True)),
            as_row(jnp.sum(mass_acc[g], axis=1, keepdims=True)),
        )

    def triple(first, second, third):
        wide = [jnp.broadcast_to(r, (8, BLK)) for r in (first, second, third)]
        return jnp.where(sublane == 0, wide[0], jnp.where(sublane == 1, wide[1], wide[2]))

    base = (y * (NX * NZ * NC) + v) * VN
    lane = (lax.broadcasted_iota(jnp.int32, (HALF, BLK), 1) + base).astype(F32)
    for q in range(NY):
        label_at[pl.ds(q * ROWS, ROWS)] = as_column(label_ref[pl.ds(q, 1)].astype(F32))

    def settle(u, h):
        arrived([second_copy(u, h, d) for d in (1, 2, 3)])
        q = z if h == 0 else x
        rows = group_rows(u // 2, (u % 2) * CHUNK + h * HALF, HALF)
        label_here = label_at[rows]
        acc = jnp.zeros((HALF, BLK), F32)
        for b in range(PER):
            here = out2[u, h, q, b].astype(F32)
            for d in range(3):
                here = here + in2[u, h, d, b].astype(F32)
            columns = pl.ds(b * BLK, BLK)
            hit = (label_here == lane + float(b * BLK)).astype(F32)
            here = here + hit
            target[rows, columns] = here
            acc = acc + here * logits[rows, columns]
        rest[rows] = acc

    def settle_all(*units):
        for u in units:
            for h in (0, 1):
                settle(u, h)

    def gradients(first, count):
        def piece(t, carry):
            rows = pl.ds(pl.multiple_of(t * 32, 32), 32)
            log_here, mass_here = log_total[rows], mass_plus[rows]
            for b in range(PER):
                columns = pl.ds(b * BLK, BLK)
                grad = mass_here * jnp.exp(logits[rows, columns] - log_here) - target[rows, columns]
                grad_ref[rows, columns] = grad.astype(BF16)
            return carry

        lax.fori_loop(first, first + count, piece, 0)

    def joined3(parts):
        best = functools.reduce(jnp.maximum, [p[0:1] for p in parts])
        exps = functools.reduce(jnp.add, [p[1:2] * jnp.exp(p[0:1] - best) for p in parts])
        mass = functools.reduce(jnp.add, [p[2:3] for p in parts])
        return triple(best, exps, mass)

    def combine(out, own, into, count):
        for q in range(NY):
            out[q] = joined3([own[q]] + [into[i, q] for i in range(count)])

    def loss_part(g):
        column = jnp.sum(rest[group_rows(g)], axis=1, keepdims=True)
        f1_out[g] = jnp.broadcast_to(as_row(column), (8, BLK))

    def loss_copy(g):
        return remote(f1_out.at[g], f1_in.at[g - 1], f1_send.at[g - 1], f1_recv.at[g - 1],
                      along_y(NY - g))

    contribute(0, 0)
    contribute(0, 1)
    arrived(raw_copies[0:2])
    start(raw_copies[2:4])
    arrived(t3_copies)
    contribute(1, 0)
    contribute(3, 1)
    arrived(mask_copies)
    merge_all(0, 1)
    arrived(raw_copies[2:4])
    start(raw_copies[4:6])
    contribute(1, 1)
    contribute(3, 0)
    load_hidden.wait()
    load_head.wait()
    merge_all(2, 7)
    arrived(raw_copies[4:6])
    start(hidden_copies[0:4])
    contribute(2, 0)
    contribute(2, 1)
    student(0)
    merge_all(3, 6)
    arrived(hidden_copies[0:4])
    start(hidden_copies[4:6])
    sibling_copies = [sibling_copy(d) for d in (1, 3, 2)]
    start(sibling_copies[:2])
    arrived(sibling_copies[:2])
    student(1)
    student(3)
    arrived(hidden_copies[4:6])
    start(sibling_copies[2:])
    arrived(sibling_copies[2:])
    student(2)
    keep = pltpu.make_async_copy(hidden, everyone_hbm, local_sem.at[4])
    keep.start()

    copies = stage_y(a1_out, a1_in, a1_send, a1_recv)
    start(copies)
    settle_all(0, 1)
    arrived(copies)
    combine(a2_out, a1_out, a1_in, 3)
    copies = stage_x(a2_out, a2_in, a2_send, a2_recv)
    start(copies)
    merge_all(4)
    arrived(copies)
    combine(a3_out, a2_out, a2_in, 7)
    copies = stage_z(a3_out, a3_in, a3_send, a3_recv)
    start(copies)
    merge_all(5)
    settle_all(2, 7)
    arrived(copies)
    for q in range(NY):
        stats = joined3([a3_out[q]] + [a3_in[i, q] for i in range(3)])
        rows = pl.ds(q * ROWS, ROWS)
        log_total[rows] = as_column(stats[0:1] + jnp.log(stats[1:2]))
        mass_plus[rows] = as_column(stats[2:3] + 1.0)
        f1_out[q] = stats

    mine = f1_out[y]
    own_log = mine[0:1] + jnp.log(mine[1:2])
    own_terms = mine[2:3] * own_log + own_log
    settle_all(3, 6)
    for g in (0, 1, 3):
        loss_part(g)
    loss_copies = [loss_copy(g) for g in (1, 3, 2)]
    start(loss_copies[:2])
    settle_all(4, 5)
    loss_part(2)
    start(loss_copies[2:])
    gradients(0, 5)
    arrived(loss_copies)
    f2_out[...] = f1_out[0] + (f1_in[0] + f1_in[1] + f1_in[2])
    copies = stage_x(f2_out, f2_in, f2_send, f2_recv)
    start(copies)
    gradients(5, 6)
    arrived(copies)
    f3_out[...] = functools.reduce(jnp.add, [f2_out[...]] + [f2_in[i] for i in range(7)])
    copies = stage_z(f3_out, f3_in, f3_send, f3_recv)
    start(copies)
    gradients(11, 5)
    arrived(copies)
    everything = f3_out[...] + (f3_in[0] + f3_in[1] + f3_in[2])
    loss_ref[...] = own_terms - everything[0:1]

    keep.wait()
    for copy in pending:
        copy.wait_send()


def exchange(key, label, raw, hidden, head, weight):
    dma = pltpu.SemaphoreType.DMA
    vmem = pltpu.VMEM
    tile, quad = (8, BLK), (NY, 8, BLK)
    scratch = [
        vmem((NX, NZ, NC, 2, 8, BLK), F32),
        vmem((NY, ROWS, OLD * BLK), BF16),
        vmem((OLD, CHUNK, BLK), BF16),
        vmem((ENT, BLK, BLK), BF16),
        vmem((NY * ROWS, D), BF16),
        vmem((D, VN), BF16),
        vmem((NY * ROWS, VN), F32),
        vmem((NY * ROWS, VN), F32),
        vmem((NU, NX, NZ, NC, 2, CHUNK, BLK), BF16),
        vmem((NU, 2, 7, 4, 2, HALF, BLK), BF16),
        vmem((NU, 2, 4, PER, HALF, BLK), BF16),
        vmem((NU, 2, 3, PER, HALF, BLK), BF16),
        vmem((2, 7, 4, 2, 8, BLK), F32),
        vmem((NY, ROWS, BLK), F32),
        vmem((NY * ROWS, BLK), F32),
        vmem((NY * ROWS, BLK), F32),
        vmem((NY * ROWS, BLK), F32),
        vmem((NY * ROWS, BLK), F32),
        vmem(tile, F32), vmem((7,) + tile, F32),
        vmem(tile, F32), vmem((3,) + tile, F32),
        vmem(tile, F32), vmem((3,) + tile, F32),
        vmem(quad, F32), vmem((3,) + quad, F32),
        vmem(quad, F32), vmem((7,) + quad, F32),
        vmem(quad, F32), vmem((3,) + quad, F32),
        vmem(quad, F32), vmem((3,) + tile, F32),
        vmem(tile, F32), vmem((7,) + tile, F32),
        vmem(tile, F32), vmem((3,) + tile, F32),
        dma((5,)), dma((6,)), dma((6,)), dma((2, 7)), dma((2, 7)),
        dma((NU, 2, 7)), dma((NU, 2, 7)), dma((NU, 2, 3)), dma((NU, 2, 3)),
        dma((6,)), dma((6,)), dma((3,)), dma((3,)),
    ]
    for count in (7, 3, 3, 3, 7, 3, 3, 7, 3):
        scratch += [dma((count,)), dma((count,))]
    smem = pl.BlockSpec(memory_space=pltpu.SMEM)
    inside = pl.BlockSpec(memory_space=pltpu.VMEM)
    outside = pl.BlockSpec(memory_space=pl.ANY)
    return pl.pallas_call(
        exchange_kernel,
        out_shape=(
            jax.ShapeDtypeStruct((1, ROWS), F32),
            jax.ShapeDtypeStruct((NY * ROWS, VN), BF16),
            jax.ShapeDtypeStruct((NY * ROWS, D), BF16),
        ),
        in_specs=[smem, inside] + [outside] * 4,
        out_specs=(inside, inside, outside),
        scratch_shapes=scratch,
        compiler_params=pltpu.CompilerParams(
            collective_id=0, has_side_effects=True, vmem_limit_bytes=60 << 20
        ),
        name="exchange",
    )(key, label, raw, hidden, head, weight)


GRAD_ROWS = 1152


def grad_kernel(hidden_ref, grad_ref, out_ref):
    out_ref[...] = lax.dot_general(
        hidden_ref[...], grad_ref[...], (((0,), (0,)), ((), ())), preferred_element_type=F32
    ).astype(BF16)


def head_gradient(hidden, grad):
    return pl.pallas_call(
        grad_kernel,
        grid=(D // GRAD_ROWS,),
        out_shape=jax.ShapeDtypeStruct((D, VN), BF16),
        in_specs=[
            pl.BlockSpec((NY * ROWS, GRAD_ROWS), lambda i: (0, i)),
            pl.BlockSpec((NY * ROWS, VN), lambda i: (0, 0)),
        ],
        out_specs=pl.BlockSpec((GRAD_ROWS, VN), lambda i: (i, 0)),
        compiler_params=pltpu.CompilerParams(vmem_limit_bytes=60 << 20),
        name="head_gradient",
    )(hidden, grad)


def local(teacher_logits, hidden, new_head, labels, map_target, map_weight):
    y = lax.axis_index("tok")
    nodes = NX * NZ * NC
    flat = map_target.reshape(1, ENT)
    owner = flat // PER - y * nodes
    match = owner == jnp.arange(nodes, dtype=jnp.int32)[:, None]
    index = jnp.arange(ENT, dtype=jnp.int32)[None, :]
    key = index * PER + flat % PER
    none = ENT * PER
    first = jnp.min(jnp.where(match, key, none), axis=1)
    last = jnp.max(jnp.where(match, key, -1), axis=1)
    first = jnp.where(first < none, first, -1)
    keys = jnp.stack([first, jnp.where(last > first, last, -1)], axis=1).reshape(2 * nodes)
    loss, grad, everyone = exchange(
        keys, labels.reshape(NY, ROWS), teacher_logits, hidden, new_head,
        map_weight.reshape(ENT, BLK, BLK),
    )
    return loss.reshape(ROWS), head_gradient(everyone, grad)


def solution(mesh):
    return jax.shard_map(
        local,
        mesh=mesh,
        in_specs=(
            P("tok", "vocab"),
            P("tok", None),
            P(None, ("tok", "vocab")),
            P(),
            P("vocab", None),
            P("vocab", None, None, None),
        ),
        out_specs=(P("tok"), P(None, ("tok", "vocab"))),
        check_vma=False,
    )
```

```python
import functools

import jax
import jax.numpy as jnp
from jax import lax
from jax.experimental import pallas as pl
from jax.experimental.pallas import tpu as pltpu
from jax.sharding import PartitionSpec as P

MESH = pl.DeviceIdType.MESH
F32 = jnp.float32
BF16 = jnp.bfloat16

NY = 4
NX = 4
NZ = 4
NC = 2
ROWS = 128
CHUNK = 64
UNITS = [((0, 0), (0, 1)), ((1, 0), (3, 1)), ((1, 1), (3, 0)), ((2, 0), (2, 1))]
NU = len(UNITS)
BLK = 128
FAN = 4
D = 4608
HD = D // 2
VN = 1024
PER = 8
OLD = 32
ENT = OLD * FAN

FIRST = [(0, 1), (1, 0), (1, 1), (2, 0), (2, 1), (3, 0), (3, 1)]


def vocab_index(x, z, c):
    return (x * NZ + z) * NC + c


def as_row(column):
    return jnp.transpose(jnp.broadcast_to(column, (ROWS, BLK)))[0:1, :]


def as_column(row):
    return jnp.transpose(jnp.broadcast_to(row, (ROWS, BLK)))


def exchange_kernel(
    key_ref, label_ref, raw_hbm, hidden_hbm, head_hbm, weight_hbm,
    loss_ref, grad_ref, everyone_hbm,
    mask_ref, raw, prob, weight, hidden, head, logits, target, out1, in1, out2, in2, masks, mass_acc,
    log_total, mass_plus, label_at, rest, settled,
    t1_out, t1_in, t2_out, t2_in, t3_out, t3_in,
    a1_out, a1_in, a2_out, a2_in, a3_out, a3_in,
    f1_out, f1_in, f2_out, f2_in, f3_out, f3_in,
    local_sem, raw_send, raw_recv, mask_send, mask_recv, p1_send, p1_recv, p2_send, p2_recv,
    hid_send, hid_recv, sib_send, sib_recv,
    t1_send, t1_recv, t2_send, t2_recv, t3_send, t3_recv,
    a1_send, a1_recv, a2_send, a2_recv, a3_send, a3_recv,
    f1_send, f1_recv, f2_send, f2_recv, f3_send, f3_recv,
):
    y = lax.axis_index("tok")
    v = lax.axis_index("vocab")
    x = v // (NZ * NC)
    z = (v // NC) % NZ
    c = v % NC

    def remote(src, dst, send, recv, device):
        return pltpu.make_async_remote_copy(
            src_ref=src, dst_ref=dst, send_sem=send, recv_sem=recv,
            device_id=device, device_id_type=MESH,
        )

    def along_x(step, core_step=0):
        return (y, vocab_index((x + step) % NX, z, (c + core_step) % NC))

    def along_z(step, core_step=0):
        return (y, vocab_index(x, (z + step) % NZ, (c + core_step) % NC))

    def along_y(step):
        return ((y + step) % NY, v)

    load_raw = pltpu.make_async_copy(raw_hbm, raw.at[0], local_sem.at[0])
    load_weight = pltpu.make_async_copy(weight_hbm, weight, local_sem.at[1])
    own_rows = pl.ds(pl.multiple_of(y * ROWS, ROWS), ROWS)
    load_hidden = pltpu.make_async_copy(hidden_hbm, hidden.at[own_rows], local_sem.at[2])
    load_head = pltpu.make_async_copy(head_hbm, head, local_sem.at[3])
    load_raw.start()

    barrier = pltpu.get_barrier_semaphore()
    partners = [along_x(da, dc) for da, dc in FIRST]
    partners += [along_z(da, dc) for da, dc in FIRST if da]
    partners += [along_y(step) for step in (1, 2, 3)]
    for partner in partners:
        pl.semaphore_signal(barrier, inc=1, device_id=partner, device_id_type=MESH)
    pl.semaphore_wait(barrier, len(partners))

    def first_partner(h, i):
        da, dc = FIRST[i]
        return along_x(da, dc) if h == 0 else along_z(da, dc)

    def mask_copy(h, i):
        da, dc = FIRST[i]
        c2 = (c + dc) % NC
        if h == 0:
            src = mask_ref.at[(x + da) % NX, :, c2]
        else:
            src = mask_ref.at[:, (z + da) % NZ, c2]
        return remote(src, masks.at[h, i], mask_send.at[h, i], mask_recv.at[h, i],
                      first_partner(h, i))

    def first_copy(u, h, i):
        da, dc = FIRST[i]
        c2 = (c + dc) % NC
        rows = pl.ds(h * CHUNK, CHUNK)
        if h == 0:
            src = out1.at[u, (x + da) % NX, :, c2, :, rows]
        else:
            src = out1.at[u, :, (z + da) % NZ, c2, :, rows]
        return remote(src, in1.at[u, h, i], p1_send.at[u, h, i], p1_recv.at[u, h, i],
                      first_partner(h, i))

    def second_copy(u, h, d):
        if h == 0:
            q, device = (z + d) % NZ, along_z(d)
        else:
            q, device = (x + d) % NX, along_x(d)
        return remote(out2.at[u, h, q], in2.at[u, h, d - 1], p2_send.at[u, h, d - 1],
                      p2_recv.at[u, h, d - 1], device)

    upper, lower = pl.ds(0, CHUNK), pl.ds(CHUNK, CHUNK)
    raw_copies = [
        remote(raw.at[source, rows], raw.at[into, rows], raw_send.at[i], raw_recv.at[i], along_y(d))
        for i, (source, into, rows, d) in enumerate([
            (0, 1, upper, 1), (0, 3, lower, 3), (0, 1, lower, 1), (0, 3, upper, 3),
            (1, 2, upper, 1), (3, 2, lower, 3),
        ])
    ]

    own_columns = pl.ds(pl.multiple_of(c * HD, HD), HD)

    def hidden_part(d, first=0, count=ROWS):
        start_row = ((y - d + NY) % NY) * ROWS + first
        rows = pl.ds(pl.multiple_of(start_row, CHUNK), count)
        return hidden.at[rows, own_columns]

    hidden_copies = [
        remote(hidden_part(*what), hidden_part(*what), hid_send.at[i], hid_recv.at[i], along_y(d))
        for i, (what, d) in enumerate([
            ((0, 0, CHUNK), 1), ((0, CHUNK, CHUNK), 3), ((0, CHUNK, CHUNK), 1), ((0, 0, CHUNK), 3),
            ((1, 0, CHUNK), 1), ((3, CHUNK, CHUNK), 3),
        ])
    ]

    def sibling_copy(d):
        part = hidden_part(d)
        return remote(part, part, sib_send.at[d - 1], sib_recv.at[d - 1], along_x(0, 1))

    def stage_x(out, into, send, recv):
        return [remote(out, into.at[i], send.at[i], recv.at[i], first_partner(0, i))
                for i in range(7)]

    def stage_z(out, into, send, recv):
        return [remote(out, into.at[d - 1], send.at[d - 1], recv.at[d - 1], along_z(d))
                for d in (1, 2, 3)]

    def stage_y(out, into, send, recv):
        return [remote(out, into.at[d - 1], send.at[d - 1], recv.at[d - 1], along_y(d))
                for d in (1, 2, 3)]

    pending = []

    def start(copies):
        for copy in copies:
            copy.start()
        pending.extend(copies)

    def arrived(copies):
        for copy in copies:
            copy.wait_recv()

    sublane = lax.broadcasted_iota(jnp.int32, (8, BLK), 0)

    def mask_rows(o, carry):
        for k in range(2):
            key = key_ref[o * 2 + k]
            row = jnp.where(key < 0, -1, key % PER)
            mask_ref[o // (NZ * NC), (o // NC) % NZ, o % NC, k] = (sublane == row).astype(F32)
        return carry

    lax.fori_loop(0, NX * NZ * NC, mask_rows, 0, unroll=4)
    load_raw.wait()
    start(raw_copies[:2])
    load_weight.start()
    load_hidden.start()
    load_head.start()
    mask_copies = [mask_copy(h, i) for h in (0, 1) for i in range(7)]
    start(mask_copies)

    def block_max(j, acc):
        part = raw[0, :, pl.ds(pl.multiple_of(j * BLK, BLK), BLK)].astype(F32)
        return jnp.maximum(acc, part)

    top = lax.fori_loop(1, OLD, block_max, raw[0, :, pl.ds(0, BLK)].astype(F32), unroll=4)
    top = jnp.broadcast_to(jnp.max(top, axis=1, keepdims=True), (ROWS, BLK))

    def block_sum(j, acc):
        part = raw[0, :, pl.ds(pl.multiple_of(j * BLK, BLK), BLK)].astype(F32)
        return acc + jnp.exp(part - top)

    total = lax.fori_loop(0, OLD, block_sum, jnp.zeros((ROWS, BLK), F32), unroll=4)
    total = jnp.sum(total, axis=1, keepdims=True)
    def stacked(first, second):
        return jnp.where(sublane == 0, jnp.broadcast_to(first, (8, BLK)),
                         jnp.broadcast_to(second, (8, BLK)))

    def joined(pairs):
        best = functools.reduce(jnp.maximum, [p[0:1] for p in pairs])
        mass = functools.reduce(jnp.add, [p[1:2] * jnp.exp(p[0:1] - best) for p in pairs])
        return stacked(best, mass)

    t1_out[...] = stacked(as_row(top[:, 0:1]), as_row(total))
    copies = stage_x(t1_out, t1_in, t1_send, t1_recv)
    start(copies)
    arrived(copies)
    t2_out[...] = joined([t1_out[...]] + [t1_in[i] for i in range(7)])
    copies = stage_z(t2_out, t2_in, t2_send, t2_recv)
    start(copies)
    arrived(copies)
    t3_out[...] = joined([t2_out[...]] + [t2_in[i] for i in range(3)])
    t3_copies = stage_y(t3_out, t3_in, t3_send, t3_recv)
    start(t3_copies)
    load_weight.wait()

    def contribute(u):
        for h, (g, part) in enumerate(UNITS[u]):
            tokens = pl.ds(part * CHUNK, CHUNK)
            into = pl.ds(h * CHUNK, CHUNK)
            stats = t3_out[...] if g == 0 else t3_in[g - 1]
            best = as_column(stats[0:1])[part * CHUNK : (part + 1) * CHUNK]
            inverse = as_column(1.0 / stats[1:2])[part * CHUNK : (part + 1) * CHUNK]

            def normalise(j, carry):
                scores = raw[g, tokens, pl.ds(pl.multiple_of(j * BLK, BLK), BLK)].astype(F32)
                prob[j, into] = (jnp.exp(scores - best) * inverse).astype(BF16)
                return carry

            lax.fori_loop(0, OLD, normalise, 0, unroll=4)

        def slot(o, acc):
            for k in range(2):
                key = key_ref[o * 2 + k]
                e = jnp.maximum(key, 0) // PER
                filled = jnp.where(key < 0, 0.0, 1.0)
                product = jnp.dot(prob[e // FAN], weight[e], preferred_element_type=F32)
                product = product.astype(BF16)
                out1[u, o // (NZ * NC), (o // NC) % NZ, o % NC, k] = product
                acc = acc + product.astype(F32) * filled
            return acc

        acc = lax.fori_loop(0, 32, slot, jnp.zeros((2 * CHUNK, BLK), F32), unroll=2)
        for h, (g, part) in enumerate(UNITS[u]):
            mass_acc[g, pl.ds(part * CHUNK, CHUNK)] = acc[h * CHUNK : (h + 1) * CHUNK]
        start([first_copy(u, h, i) for i in range(7) for h in (0, 1)])

    def merge(u, h):
        arrived([first_copy(u, h, i) for i in range(7)])

        def piece(t, carry):
            q, rows = t // 2, pl.ds(pl.multiple_of((t % 2) * 32, 32), 32)
            own = pl.ds(pl.multiple_of(h * CHUNK + (t % 2) * 32, 32), 32)
            sums = [jnp.zeros((32, BLK), F32) for _ in range(PER)]
            for i in range(8):
                for k in range(2):
                    if i < 7:
                        part, hit = in1[u, h, i, q, k, rows], masks[h, i, q, k]
                    elif h == 0:
                        part, hit = out1[u, x, q, c, k, own], mask_ref[x, q, c, k]
                    else:
                        part, hit = out1[u, q, z, c, k, own], mask_ref[q, z, c, k]
                    part = part.astype(F32)
                    for b in range(PER):
                        sums[b] = sums[b] + part * hit[b : b + 1]
            for b in range(PER):
                out2[u, h, q, b, rows] = sums[b].astype(BF16)
            return carry

        lax.fori_loop(0, 8, piece, 0)
        start([second_copy(u, h, d) for d in (1, 2, 3)])

    def merge_all(*units):
        for u in units:
            for h in (0, 1):
                merge(u, h)

    def group_rows(g, first=0, count=ROWS):
        start_row = ((y - g + NY) % NY) * ROWS + first
        return pl.ds(pl.multiple_of(start_row, CHUNK), count)

    def student(g):
        rows = group_rows(g)

        def columns_of(n, carry):
            columns = pl.ds(pl.multiple_of(n * 256, 256), 256)
            logits[rows, columns] = jnp.dot(
                hidden[rows, :], head[:, columns], preferred_element_type=F32
            )
            return carry

        lax.fori_loop(0, VN // 256, columns_of, 0)
        best = logits[rows, pl.ds(0, BLK)]
        for b in range(1, PER):
            best = jnp.maximum(best, logits[rows, pl.ds(b * BLK, BLK)])
        best = jnp.broadcast_to(jnp.max(best, axis=1, keepdims=True), (ROWS, BLK))
        acc = jnp.zeros((ROWS, BLK), F32)
        for b in range(PER):
            acc = acc + jnp.exp(logits[rows, pl.ds(b * BLK, BLK)] - best)
        a1_out[(y - g + NY) % NY] = triple(
            as_row(best[:, 0:1]),
            as_row(jnp.sum(acc, axis=1, keepdims=True)),
            as_row(jnp.sum(mass_acc[g], axis=1, keepdims=True)),
        )

    def triple(first, second, third):
        wide = [jnp.broadcast_to(r, (8, BLK)) for r in (first, second, third)]
        return jnp.where(sublane == 0, wide[0], jnp.where(sublane == 1, wide[1], wide[2]))

    base = (y * (NX * NZ * NC) + v) * VN
    lane = (lax.broadcasted_iota(jnp.int32, (32, BLK), 1) + base).astype(F32)
    for q in range(NY):
        label_at[pl.ds(q * ROWS, ROWS)] = as_column(label_ref[pl.ds(q, 1)].astype(F32))

    def settle(u, h):
        arrived([second_copy(u, h, d) for d in (1, 2, 3)])
        q = z if h == 0 else x
        g, half = UNITS[u][h]

        def piece(t, carry):
            part = pl.ds(pl.multiple_of(t * 32, 32), 32)
            start_row = ((y - g + NY) % NY) * ROWS + half * CHUNK + t * 32
            rows = pl.ds(pl.multiple_of(start_row, 32), 32)
            label_here = label_at[rows]
            acc = jnp.zeros((32, BLK), F32)
            for b in range(PER):
                here = out2[u, h, q, b, part].astype(F32)
                for d in range(3):
                    here = here + in2[u, h, d, b, part].astype(F32)
                columns = pl.ds(b * BLK, BLK)
                hit = (label_here == lane + float(b * BLK)).astype(F32)
                here = here + hit
                target[rows, columns] = here
                acc = acc + here * logits[rows, columns]
            rest[rows] = acc
            return carry

        lax.fori_loop(0, CHUNK // 32, piece, 0)

    def settle_all(*units):
        for u in units:
            for h in (0, 1):
                settle(u, h)

    def gradients(first, count):
        def piece(t, carry):
            rows = pl.ds(pl.multiple_of(t * 32, 32), 32)
            log_here, mass_here = log_total[rows], mass_plus[rows]
            for b in range(PER):
                columns = pl.ds(b * BLK, BLK)
                grad = mass_here * jnp.exp(logits[rows, columns] - log_here) - target[rows, columns]
                grad_ref[rows, columns] = grad.astype(BF16)
            return carry

        lax.fori_loop(first, first + count, piece, 0)

    def joined3(parts):
        best = functools.reduce(jnp.maximum, [p[0:1] for p in parts])
        exps = functools.reduce(jnp.add, [p[1:2] * jnp.exp(p[0:1] - best) for p in parts])
        mass = functools.reduce(jnp.add, [p[2:3] for p in parts])
        return triple(best, exps, mass)

    def combine(out, own, into, count):
        for q in range(NY):
            out[q] = joined3([own[q]] + [into[i, q] for i in range(count)])

    def loss_part(g):
        column = jnp.sum(rest[group_rows(g)], axis=1, keepdims=True)
        f1_out[g] = jnp.broadcast_to(as_row(column), (8, BLK))

    def loss_copy(g):
        return remote(f1_out.at[g], f1_in.at[g - 1], f1_send.at[g - 1], f1_recv.at[g - 1],
                      along_y(NY - g))

    contribute(0)
    arrived(raw_copies[0:2])
    start(raw_copies[2:4])
    arrived(t3_copies)
    contribute(1)
    arrived(mask_copies)
    merge_all(0)
    arrived(raw_copies[2:4])
    start(raw_copies[4:6])
    contribute(2)
    load_hidden.wait()
    load_head.wait()
    merge_all(1)
    arrived(raw_copies[4:6])
    start(hidden_copies[0:4])
    contribute(3)
    student(0)
    merge_all(2)
    arrived(hidden_copies[0:4])
    start(hidden_copies[4:6])
    sibling_copies = [sibling_copy(d) for d in (1, 3, 2)]
    start(sibling_copies[:2])
    settle_all(0)
    arrived(sibling_copies[:2])
    student(1)
    merge_all(3)
    student(3)
    arrived(hidden_copies[4:6])
    start(sibling_copies[2:])
    arrived(sibling_copies[2:])
    student(2)
    keep = pltpu.make_async_copy(hidden, everyone_hbm, local_sem.at[4])
    keep.start()

    copies = stage_y(a1_out, a1_in, a1_send, a1_recv)
    start(copies)
    settle_all(1)
    arrived(copies)
    combine(a2_out, a1_out, a1_in, 3)
    copies = stage_x(a2_out, a2_in, a2_send, a2_recv)
    start(copies)
    settle_all(2)
    for g in (0, 1, 3):
        loss_part(g)
    loss_copies = [loss_copy(g) for g in (1, 3, 2)]
    start(loss_copies[:2])
    arrived(copies)
    combine(a3_out, a2_out, a2_in, 7)
    copies = stage_z(a3_out, a3_in, a3_send, a3_recv)
    start(copies)
    settle_all(3)
    loss_part(2)
    start(loss_copies[2:])
    arrived(copies)
    for q in range(NY):
        stats = joined3([a3_out[q]] + [a3_in[i, q] for i in range(3)])
        rows = pl.ds(q * ROWS, ROWS)
        log_total[rows] = as_column(stats[0:1] + jnp.log(stats[1:2]))
        mass_plus[rows] = as_column(stats[2:3] + 1.0)
        settled[q] = stats

    mine = settled[y]
    own_log = mine[0:1] + jnp.log(mine[1:2])
    own_terms = mine[2:3] * own_log + own_log
    gradients(0, 5)
    arrived(loss_copies)
    f2_out[...] = f1_out[0] + (f1_in[0] + f1_in[1] + f1_in[2])
    copies = stage_x(f2_out, f2_in, f2_send, f2_recv)
    start(copies)
    gradients(5, 6)
    arrived(copies)
    f3_out[...] = functools.reduce(jnp.add, [f2_out[...]] + [f2_in[i] for i in range(7)])
    copies = stage_z(f3_out, f3_in, f3_send, f3_recv)
    start(copies)
    gradients(11, 5)
    arrived(copies)
    everything = f3_out[...] + (f3_in[0] + f3_in[1] + f3_in[2])
    loss_ref[...] = own_terms - everything[0:1]

    keep.wait()
    for copy in pending:
        copy.wait_send()


def exchange(key, label, raw, hidden, head, weight):
    dma = pltpu.SemaphoreType.DMA
    vmem = pltpu.VMEM
    tile, quad = (8, BLK), (NY, 8, BLK)
    scratch = [
        vmem((NX, NZ, NC, 2, 8, BLK), F32),
        vmem((NY, ROWS, OLD * BLK), BF16),
        vmem((OLD, 2 * CHUNK, BLK), BF16),
        vmem((ENT, BLK, BLK), BF16),
        vmem((NY * ROWS, D), BF16),
        vmem((D, VN), BF16),
        vmem((NY * ROWS, VN), F32),
        vmem((NY * ROWS, VN), F32),
        vmem((NU, NX, NZ, NC, 2, 2 * CHUNK, BLK), BF16),
        vmem((NU, 2, 7, 4, 2, CHUNK, BLK), BF16),
        vmem((NU, 2, 4, PER, CHUNK, BLK), BF16),
        vmem((NU, 2, 3, PER, CHUNK, BLK), BF16),
        vmem((2, 7, 4, 2, 8, BLK), F32),
        vmem((NY, ROWS, BLK), F32),
        vmem((NY * ROWS, BLK), F32),
        vmem((NY * ROWS, BLK), F32),
        vmem((NY * ROWS, BLK), F32),
        vmem((NY * ROWS, BLK), F32),
        vmem(quad, F32),
        vmem(tile, F32), vmem((7,) + tile, F32),
        vmem(tile, F32), vmem((3,) + tile, F32),
        vmem(tile, F32), vmem((3,) + tile, F32),
        vmem(quad, F32), vmem((3,) + quad, F32),
        vmem(quad, F32), vmem((7,) + quad, F32),
        vmem(quad, F32), vmem((3,) + quad, F32),
        vmem(quad, F32), vmem((3,) + tile, F32),
        vmem(tile, F32), vmem((7,) + tile, F32),
        vmem(tile, F32), vmem((3,) + tile, F32),
        dma((5,)), dma((6,)), dma((6,)), dma((2, 7)), dma((2, 7)),
        dma((NU, 2, 7)), dma((NU, 2, 7)), dma((NU, 2, 3)), dma((NU, 2, 3)),
        dma((6,)), dma((6,)), dma((3,)), dma((3,)),
    ]
    for count in (7, 3, 3, 3, 7, 3, 3, 7, 3):
        scratch += [dma((count,)), dma((count,))]
    smem = pl.BlockSpec(memory_space=pltpu.SMEM)
    inside = pl.BlockSpec(memory_space=pltpu.VMEM)
    outside = pl.BlockSpec(memory_space=pl.ANY)
    return pl.pallas_call(
        exchange_kernel,
        out_shape=(
            jax.ShapeDtypeStruct((1, ROWS), F32),
            jax.ShapeDtypeStruct((NY * ROWS, VN), BF16),
            jax.ShapeDtypeStruct((NY * ROWS, D), BF16),
        ),
        in_specs=[smem, inside] + [outside] * 4,
        out_specs=(inside, inside, outside),
        scratch_shapes=scratch,
        compiler_params=pltpu.CompilerParams(
            collective_id=0, has_side_effects=True, vmem_limit_bytes=60 << 20
        ),
        name="exchange",
    )(key, label, raw, hidden, head, weight)


GRAD_ROWS = 1152


def grad_kernel(hidden_ref, grad_ref, out_ref):
    out_ref[...] = lax.dot_general(
        hidden_ref[...], grad_ref[...], (((0,), (0,)), ((), ())), preferred_element_type=F32
    ).astype(BF16)


def head_gradient(hidden, grad):
    return pl.pallas_call(
        grad_kernel,
        grid=(D // GRAD_ROWS,),
        out_shape=jax.ShapeDtypeStruct((D, VN), BF16),
        in_specs=[
            pl.BlockSpec((NY * ROWS, GRAD_ROWS), lambda i: (0, i)),
            pl.BlockSpec((NY * ROWS, VN), lambda i: (0, 0)),
        ],
        out_specs=pl.BlockSpec((GRAD_ROWS, VN), lambda i: (i, 0)),
        compiler_params=pltpu.CompilerParams(vmem_limit_bytes=60 << 20),
        name="head_gradient",
    )(hidden, grad)


def local(teacher_logits, hidden, new_head, labels, map_target, map_weight):
    y = lax.axis_index("tok")
    nodes = NX * NZ * NC
    flat = map_target.reshape(1, ENT)
    owner = flat // PER - y * nodes
    match = owner == jnp.arange(nodes, dtype=jnp.int32)[:, None]
    index = jnp.arange(ENT, dtype=jnp.int32)[None, :]
    key = index * PER + flat % PER
    none = ENT * PER
    first = jnp.min(jnp.where(match, key, none), axis=1)
    last = jnp.max(jnp.where(match, key, -1), axis=1)
    first = jnp.where(first < none, first, -1)
    keys = jnp.stack([first, jnp.where(last > first, last, -1)], axis=1).reshape(2 * nodes)
    loss, grad, everyone = exchange(
        keys, labels.reshape(NY, ROWS), teacher_logits, hidden, new_head,
        map_weight.reshape(ENT, BLK, BLK),
    )
    return loss.reshape(ROWS), head_gradient(everyone, grad)


def solution(mesh):
    return jax.shard_map(
        local,
        mesh=mesh,
        in_specs=(
            P("tok", "vocab"),
            P("tok", None),
            P(None, ("tok", "vocab")),
            P(),
            P("vocab", None),
            P("vocab", None, None, None),
        ),
        out_specs=(P("tok"), P(None, ("tok", "vocab"))),
        check_vma=False,
    )
```

```python
import functools

import jax
import jax.numpy as jnp
from jax import lax
from jax.experimental import pallas as pl
from jax.experimental.pallas import tpu as pltpu
from jax.sharding import PartitionSpec as P

MESH = pl.DeviceIdType.MESH
F32 = jnp.float32
BF16 = jnp.bfloat16

NY = 4
NX = 4
NZ = 4
NC = 2
ROWS = 128
CHUNK = 64
HALF = CHUNK // 2
NU = NY * ROWS // CHUNK
BLK = 128
FAN = 4
D = 4608
HD = D // 2
VN = 1024
PER = 8
OLD = 32
ENT = OLD * FAN

FIRST = [(0, 1), (1, 0), (1, 1), (2, 0), (2, 1), (3, 0), (3, 1)]


def vocab_index(x, z, c):
    return (x * NZ + z) * NC + c


def as_row(column):
    return jnp.transpose(jnp.broadcast_to(column, (ROWS, BLK)))[0:1, :]


def as_column(row):
    return jnp.transpose(jnp.broadcast_to(row, (ROWS, BLK)))


def exchange_kernel(
    key_ref, label_ref, raw_hbm, hidden_hbm, head_hbm, weight_hbm,
    loss_ref, grad_ref, everyone_hbm,
    mask_ref, raw, prob, weight, hidden, head, logits, target, out1, in1, out2, in2, masks, mass_acc,
    log_total, mass_plus, label_at, rest,
    t1_out, t1_in, t2_out, t2_in, t3_out, t3_in,
    a1_out, a1_in, a2_out, a2_in, a3_out, a3_in,
    f1_out, f1_in, f2_out, f2_in, f3_out, f3_in,
    local_sem, raw_send, raw_recv, mask_send, mask_recv, p1_send, p1_recv, p2_send, p2_recv,
    hid_send, hid_recv, sib_send, sib_recv,
    t1_send, t1_recv, t2_send, t2_recv, t3_send, t3_recv,
    a1_send, a1_recv, a2_send, a2_recv, a3_send, a3_recv,
    f1_send, f1_recv, f2_send, f2_recv, f3_send, f3_recv,
):
    y = lax.axis_index("tok")
    v = lax.axis_index("vocab")
    x = v // (NZ * NC)
    z = (v // NC) % NZ
    c = v % NC

    def remote(src, dst, send, recv, device):
        return pltpu.make_async_remote_copy(
            src_ref=src, dst_ref=dst, send_sem=send, recv_sem=recv,
            device_id=device, device_id_type=MESH,
        )

    def along_x(step, core_step=0):
        return (y, vocab_index((x + step) % NX, z, (c + core_step) % NC))

    def along_z(step, core_step=0):
        return (y, vocab_index(x, (z + step) % NZ, (c + core_step) % NC))

    def along_y(step):
        return ((y + step) % NY, v)

    load_raw = pltpu.make_async_copy(raw_hbm, raw.at[0], local_sem.at[0])
    load_weight = pltpu.make_async_copy(weight_hbm, weight, local_sem.at[1])
    own_rows = pl.ds(pl.multiple_of(y * ROWS, ROWS), ROWS)
    load_hidden = pltpu.make_async_copy(hidden_hbm, hidden.at[own_rows], local_sem.at[2])
    load_head = pltpu.make_async_copy(head_hbm, head, local_sem.at[3])
    load_raw.start()

    barrier = pltpu.get_barrier_semaphore()
    partners = [along_x(da, dc) for da, dc in FIRST]
    partners += [along_z(da, dc) for da, dc in FIRST if da]
    partners += [along_y(step) for step in (1, 2, 3)]
    for partner in partners:
        pl.semaphore_signal(barrier, inc=1, device_id=partner, device_id_type=MESH)
    pl.semaphore_wait(barrier, len(partners))

    def first_partner(h, i):
        da, dc = FIRST[i]
        return along_x(da, dc) if h == 0 else along_z(da, dc)

    def mask_copy(h, i):
        da, dc = FIRST[i]
        c2 = (c + dc) % NC
        if h == 0:
            src = mask_ref.at[(x + da) % NX, :, c2]
        else:
            src = mask_ref.at[:, (z + da) % NZ, c2]
        return remote(src, masks.at[h, i], mask_send.at[h, i], mask_recv.at[h, i],
                      first_partner(h, i))

    def first_copy(u, h, i):
        da, dc = FIRST[i]
        c2 = (c + dc) % NC
        rows = pl.ds(h * HALF, HALF)
        if h == 0:
            src = out1.at[u, (x + da) % NX, :, c2, :, rows]
        else:
            src = out1.at[u, :, (z + da) % NZ, c2, :, rows]
        return remote(src, in1.at[u, h, i], p1_send.at[u, h, i], p1_recv.at[u, h, i],
                      first_partner(h, i))

    def second_copy(u, h, d):
        if h == 0:
            q, device = (z + d) % NZ, along_z(d)
        else:
            q, device = (x + d) % NX, along_x(d)
        return remote(out2.at[u, h, q], in2.at[u, h, d - 1], p2_send.at[u, h, d - 1],
                      p2_recv.at[u, h, d - 1], device)

    upper, lower = pl.ds(0, CHUNK), pl.ds(CHUNK, CHUNK)
    raw_copies = [
        remote(raw.at[source, rows], raw.at[into, rows], raw_send.at[i], raw_recv.at[i], along_y(d))
        for i, (source, into, rows, d) in enumerate([
            (0, 1, upper, 1), (0, 3, lower, 3), (0, 1, lower, 1), (0, 3, upper, 3),
            (1, 2, upper, 1), (3, 2, lower, 3),
        ])
    ]

    own_columns = pl.ds(pl.multiple_of(c * HD, HD), HD)

    def hidden_part(d, first=0, count=ROWS):
        start_row = ((y - d + NY) % NY) * ROWS + first
        rows = pl.ds(pl.multiple_of(start_row, CHUNK), count)
        return hidden.at[rows, own_columns]

    hidden_copies = [
        remote(hidden_part(*what), hidden_part(*what), hid_send.at[i], hid_recv.at[i], along_y(d))
        for i, (what, d) in enumerate([
            ((0, 0, CHUNK), 1), ((0, CHUNK, CHUNK), 3), ((0, CHUNK, CHUNK), 1), ((0, 0, CHUNK), 3),
            ((1, 0, CHUNK), 1), ((3, CHUNK, CHUNK), 3),
        ])
    ]

    def sibling_copy(d):
        part = hidden_part(d)
        return remote(part, part, sib_send.at[d - 1], sib_recv.at[d - 1], along_x(0, 1))

    def stage_x(out, into, send, recv):
        return [remote(out, into.at[i], send.at[i], recv.at[i], first_partner(0, i))
                for i in range(7)]

    def stage_z(out, into, send, recv):
        return [remote(out, into.at[d - 1], send.at[d - 1], recv.at[d - 1], along_z(d))
                for d in (1, 2, 3)]

    def stage_y(out, into, send, recv):
        return [remote(out, into.at[d - 1], send.at[d - 1], recv.at[d - 1], along_y(d))
                for d in (1, 2, 3)]

    pending = []

    def start(copies):
        for copy in copies:
            copy.start()
        pending.extend(copies)

    def arrived(copies):
        for copy in copies:
            copy.wait_recv()

    sublane = lax.broadcasted_iota(jnp.int32, (8, BLK), 0)

    def mask_rows(o, carry):
        for k in range(2):
            key = key_ref[o * 2 + k]
            row = jnp.where(key < 0, -1, key % PER)
            mask_ref[o // (NZ * NC), (o // NC) % NZ, o % NC, k] = (sublane == row).astype(F32)
        return carry

    load_raw.wait()
    start(raw_copies[:2])
    load_weight.start()
    load_hidden.start()
    load_head.start()

    def block_max(j, acc):
        part = raw[0, :, pl.ds(pl.multiple_of(j * BLK, BLK), BLK)].astype(F32)
        return jnp.maximum(acc, part)

    top = lax.fori_loop(1, OLD, block_max, raw[0, :, pl.ds(0, BLK)].astype(F32), unroll=4)
    top = jnp.broadcast_to(jnp.max(top, axis=1, keepdims=True), (ROWS, BLK))

    def block_sum(j, acc):
        part = raw[0, :, pl.ds(pl.multiple_of(j * BLK, BLK), BLK)].astype(F32)
        return acc + jnp.exp(part - top)

    total = lax.fori_loop(0, OLD, block_sum, jnp.zeros((ROWS, BLK), F32), unroll=4)
    total = jnp.sum(total, axis=1, keepdims=True)
    def stacked(first, second):
        return jnp.where(sublane == 0, jnp.broadcast_to(first, (8, BLK)),
                         jnp.broadcast_to(second, (8, BLK)))

    def joined(pairs):
        best = functools.reduce(jnp.maximum, [p[0:1] for p in pairs])
        mass = functools.reduce(jnp.add, [p[1:2] * jnp.exp(p[0:1] - best) for p in pairs])
        return stacked(best, mass)

    t1_out[...] = stacked(as_row(top[:, 0:1]), as_row(total))
    copies = stage_x(t1_out, t1_in, t1_send, t1_recv)
    start(copies)
    lax.fori_loop(0, NX * NZ * NC, mask_rows, 0, unroll=4)
    mask_copies = [mask_copy(h, i) for h in (0, 1) for i in range(7)]
    start(mask_copies)
    arrived(copies)
    t2_out[...] = joined([t1_out[...]] + [t1_in[i] for i in range(7)])
    copies = stage_z(t2_out, t2_in, t2_send, t2_recv)
    start(copies)
    arrived(copies)
    t3_out[...] = joined([t2_out[...]] + [t2_in[i] for i in range(3)])
    t3_copies = stage_y(t3_out, t3_in, t3_send, t3_recv)
    start(t3_copies)
    load_weight.wait()

    def contribute(g, part):
        u = g * 2 + part
        tokens = pl.ds(part * CHUNK, CHUNK)
        stats = t3_out[...] if g == 0 else t3_in[g - 1]
        best = as_column(stats[0:1])[part * CHUNK : (part + 1) * CHUNK]
        inverse = as_column(1.0 / stats[1:2])[part * CHUNK : (part + 1) * CHUNK]

        def normalise(j, carry):
            scores = raw[g, tokens, pl.ds(pl.multiple_of(j * BLK, BLK), BLK)].astype(F32)
            prob[j] = (jnp.exp(scores - best) * inverse).astype(BF16)
            return carry

        lax.fori_loop(0, OLD, normalise, 0, unroll=4)

        def slot(o, acc):
            for k in range(2):
                key = key_ref[o * 2 + k]
                e = jnp.maximum(key, 0) // PER
                filled = jnp.where(key < 0, 0.0, 1.0)
                product = jnp.dot(prob[e // FAN], weight[e], preferred_element_type=F32)
                product = product.astype(BF16)
                out1[u, o // (NZ * NC), (o // NC) % NZ, o % NC, k] = product
                acc = acc + product.astype(F32) * filled
            return acc

        acc = lax.fori_loop(0, 32, slot, jnp.zeros((CHUNK, BLK), F32), unroll=4)
        mass_acc[g, tokens] = acc
        start([first_copy(u, h, i) for i in range(7) for h in (0, 1)])

    def merge(u, h):
        arrived([first_copy(u, h, i) for i in range(7)])
        own = pl.ds(h * HALF, HALF)

        def piece(q, carry):
            sums = [jnp.zeros((HALF, BLK), F32) for _ in range(PER)]
            for i in range(8):
                for k in range(2):
                    if i < 7:
                        part, hit = in1[u, h, i, q, k], masks[h, i, q, k]
                    elif h == 0:
                        part, hit = out1[u, x, q, c, k, own], mask_ref[x, q, c, k]
                    else:
                        part, hit = out1[u, q, z, c, k, own], mask_ref[q, z, c, k]
                    part = part.astype(F32)
                    for b in range(PER):
                        sums[b] = sums[b] + part * hit[b : b + 1]
            for b in range(PER):
                out2[u, h, q, b] = sums[b].astype(BF16)
            return carry

        lax.fori_loop(0, 4, piece, 0)
        start([second_copy(u, h, d) for d in (1, 2, 3)])

    def merge_all(*units):
        for u in units:
            for h in (0, 1):
                merge(u, h)

    def group_rows(g, first=0, count=ROWS):
        start_row = ((y - g + NY) % NY) * ROWS + first
        return pl.ds(pl.multiple_of(start_row, HALF), count)

    def student(g):
        rows = group_rows(g)

        def columns_of(n, carry):
            columns = pl.ds(pl.multiple_of(n * 256, 256), 256)
            logits[rows, columns] = jnp.dot(
                hidden[rows, :], head[:, columns], preferred_element_type=F32
            )
            return carry

        lax.fori_loop(0, VN // 256, columns_of, 0)
        best = logits[rows, pl.ds(0, BLK)]
        for b in range(1, PER):
            best = jnp.maximum(best, logits[rows, pl.ds(b * BLK, BLK)])
        best = jnp.broadcast_to(jnp.max(best, axis=1, keepdims=True), (ROWS, BLK))
        acc = jnp.zeros((ROWS, BLK), F32)
        for b in range(PER):
            acc = acc + jnp.exp(logits[rows, pl.ds(b * BLK, BLK)] - best)
        a1_out[(y - g + NY) % NY] = triple(
            as_row(best[:, 0:1]),
            as_row(jnp.sum(acc, axis=1, keepdims=True)),
            as_row(jnp.sum(mass_acc[g], axis=1, keepdims=True)),
        )

    def triple(first, second, third):
        wide = [jnp.broadcast_to(r, (8, BLK)) for r in (first, second, third)]
        return jnp.where(sublane == 0, wide[0], jnp.where(sublane == 1, wide[1], wide[2]))

    base = (y * (NX * NZ * NC) + v) * VN
    lane = (lax.broadcasted_iota(jnp.int32, (HALF, BLK), 1) + base).astype(F32)

    def settle(u, h):
        arrived([second_copy(u, h, d) for d in (1, 2, 3)])
        q = z if h == 0 else x
        rows = group_rows(u // 2, (u % 2) * CHUNK + h * HALF, HALF)
        label_here = label_at[rows]
        acc = jnp.zeros((HALF, BLK), F32)
        for b in range(PER):
            here = out2[u, h, q, b].astype(F32)
            for d in range(3):
                here = here + in2[u, h, d, b].astype(F32)
            columns = pl.ds(b * BLK, BLK)
            hit = (label_here == lane + float(b * BLK)).astype(F32)
            here = here + hit
            target[rows, columns] = here
            acc = acc + here * logits[rows, columns]
        rest[rows] = acc

    def settle_all(*units):
        for u in units:
            for h in (0, 1):
                settle(u, h)

    def gradients(first, count):
        def piece(t, carry):
            rows = pl.ds(pl.multiple_of(t * 32, 32), 32)
            log_here, mass_here = log_total[rows], mass_plus[rows]
            for b in range(PER):
                columns = pl.ds(b * BLK, BLK)
                grad = mass_here * jnp.exp(logits[rows, columns] - log_here) - target[rows, columns]
                grad_ref[rows, columns] = grad.astype(BF16)
            return carry

        lax.fori_loop(first, first + count, piece, 0)

    def joined3(parts):
        best = functools.reduce(jnp.maximum, [p[0:1] for p in parts])
        exps = functools.reduce(jnp.add, [p[1:2] * jnp.exp(p[0:1] - best) for p in parts])
        mass = functools.reduce(jnp.add, [p[2:3] for p in parts])
        return triple(best, exps, mass)

    def combine(out, own, into, count):
        for q in range(NY):
            out[q] = joined3([own[q]] + [into[i, q] for i in range(count)])

    def loss_part(g):
        column = jnp.sum(rest[group_rows(g)], axis=1, keepdims=True)
        f1_out[g] = jnp.broadcast_to(as_row(column), (8, BLK))

    def loss_copy(g):
        return remote(f1_out.at[g], f1_in.at[g - 1], f1_send.at[g - 1], f1_recv.at[g - 1],
                      along_y(NY - g))

    contribute(0, 0)
    contribute(0, 1)
    arrived(raw_copies[0:2])
    start(raw_copies[2:4])
    arrived(t3_copies)
    contribute(1, 0)
    contribute(3, 1)
    arrived(mask_copies)
    merge_all(0, 1)
    arrived(raw_copies[2:4])
    start(raw_copies[4:6])
    contribute(1, 1)
    contribute(3, 0)
    load_hidden.wait()
    load_head.wait()
    merge_all(2, 7)
    arrived(raw_copies[4:6])
    start(hidden_copies[0:4])
    contribute(2, 0)
    contribute(2, 1)
    for q in range(NY):
        label_at[pl.ds(q * ROWS, ROWS)] = as_column(label_ref[pl.ds(q, 1)].astype(F32))
    student(0)
    merge_all(3, 6)
    arrived(hidden_copies[0:4])
    start(hidden_copies[4:6])
    sibling_copies = [sibling_copy(d) for d in (1, 3, 2)]
    start(sibling_copies[:2])
    arrived(sibling_copies[:2])
    student(1)
    student(3)
    arrived(hidden_copies[4:6])
    start(sibling_copies[2:])
    arrived(sibling_copies[2:])
    student(2)
    keep = pltpu.make_async_copy(hidden, everyone_hbm, local_sem.at[4])
    keep.start()

    copies = stage_y(a1_out, a1_in, a1_send, a1_recv)
    start(copies)
    settle_all(0, 1)
    arrived(copies)
    combine(a2_out, a1_out, a1_in, 3)
    copies = stage_x(a2_out, a2_in, a2_send, a2_recv)
    start(copies)
    merge_all(4)
    arrived(copies)
    combine(a3_out, a2_out, a2_in, 7)
    copies = stage_z(a3_out, a3_in, a3_send, a3_recv)
    start(copies)
    merge_all(5)
    settle_all(2, 7)
    arrived(copies)
    for q in range(NY):
        stats = joined3([a3_out[q]] + [a3_in[i, q] for i in range(3)])
        rows = pl.ds(q * ROWS, ROWS)
        log_total[rows] = as_column(stats[0:1] + jnp.log(stats[1:2]))
        mass_plus[rows] = as_column(stats[2:3] + 1.0)
        f1_out[q] = stats

    mine = f1_out[y]
    own_log = mine[0:1] + jnp.log(mine[1:2])
    own_terms = mine[2:3] * own_log + own_log
    settle_all(3, 6)
    for g in (0, 1, 3):
        loss_part(g)
    loss_copies = [loss_copy(g) for g in (1, 3, 2)]
    start(loss_copies[:2])
    settle_all(4, 5)
    loss_part(2)
    start(loss_copies[2:])
    gradients(0, 5)
    arrived(loss_copies)
    f2_out[...] = f1_out[0] + (f1_in[0] + f1_in[1] + f1_in[2])
    copies = stage_x(f2_out, f2_in, f2_send, f2_recv)
    start(copies)
    gradients(5, 6)
    arrived(copies)
    f3_out[...] = functools.reduce(jnp.add, [f2_out[...]] + [f2_in[i] for i in range(7)])
    copies = stage_z(f3_out, f3_in, f3_send, f3_recv)
    start(copies)
    gradients(11, 5)
    arrived(copies)
    everything = f3_out[...] + (f3_in[0] + f3_in[1] + f3_in[2])
    loss_ref[...] = own_terms - everything[0:1]

    keep.wait()
    for copy in pending:
        copy.wait_send()


def exchange(key, label, raw, hidden, head, weight):
    dma = pltpu.SemaphoreType.DMA
    vmem = pltpu.VMEM
    tile, quad = (8, BLK), (NY, 8, BLK)
    scratch = [
        vmem((NX, NZ, NC, 2, 8, BLK), F32),
        vmem((NY, ROWS, OLD * BLK), BF16),
        vmem((OLD, CHUNK, BLK), BF16),
        vmem((ENT, BLK, BLK), BF16),
        vmem((NY * ROWS, D), BF16),
        vmem((D, VN), BF16),
        vmem((NY * ROWS, VN), F32),
        vmem((NY * ROWS, VN), F32),
        vmem((NU, NX, NZ, NC, 2, CHUNK, BLK), BF16),
        vmem((NU, 2, 7, 4, 2, HALF, BLK), BF16),
        vmem((NU, 2, 4, PER, HALF, BLK), BF16),
        vmem((NU, 2, 3, PER, HALF, BLK), BF16),
        vmem((2, 7, 4, 2, 8, BLK), F32),
        vmem((NY, ROWS, BLK), F32),
        vmem((NY * ROWS, BLK), F32),
        vmem((NY * ROWS, BLK), F32),
        vmem((NY * ROWS, BLK), F32),
        vmem((NY * ROWS, BLK), F32),
        vmem(tile, F32), vmem((7,) + tile, F32),
        vmem(tile, F32), vmem((3,) + tile, F32),
        vmem(tile, F32), vmem((3,) + tile, F32),
        vmem(quad, F32), vmem((3,) + quad, F32),
        vmem(quad, F32), vmem((7,) + quad, F32),
        vmem(quad, F32), vmem((3,) + quad, F32),
        vmem(quad, F32), vmem((3,) + tile, F32),
        vmem(tile, F32), vmem((7,) + tile, F32),
        vmem(tile, F32), vmem((3,) + tile, F32),
        dma((5,)), dma((6,)), dma((6,)), dma((2, 7)), dma((2, 7)),
        dma((NU, 2, 7)), dma((NU, 2, 7)), dma((NU, 2, 3)), dma((NU, 2, 3)),
        dma((6,)), dma((6,)), dma((3,)), dma((3,)),
    ]
    for count in (7, 3, 3, 3, 7, 3, 3, 7, 3):
        scratch += [dma((count,)), dma((count,))]
    smem = pl.BlockSpec(memory_space=pltpu.SMEM)
    inside = pl.BlockSpec(memory_space=pltpu.VMEM)
    outside = pl.BlockSpec(memory_space=pl.ANY)
    return pl.pallas_call(
        exchange_kernel,
        out_shape=(
            jax.ShapeDtypeStruct((1, ROWS), F32),
            jax.ShapeDtypeStruct((NY * ROWS, VN), BF16),
            jax.ShapeDtypeStruct((NY * ROWS, D), BF16),
        ),
        in_specs=[smem, inside] + [outside] * 4,
        out_specs=(inside, inside, outside),
        scratch_shapes=scratch,
        compiler_params=pltpu.CompilerParams(
            collective_id=0, has_side_effects=True, vmem_limit_bytes=60 << 20
        ),
        name="exchange",
    )(key, label, raw, hidden, head, weight)


GRAD_ROWS = 1536


def grad_kernel(hidden_ref, grad_ref, out_ref):
    out_ref[...] = lax.dot_general(
        hidden_ref[...], grad_ref[...], (((0,), (0,)), ((), ())), preferred_element_type=F32
    ).astype(BF16)


def head_gradient(hidden, grad):
    return pl.pallas_call(
        grad_kernel,
        grid=(D // GRAD_ROWS,),
        out_shape=jax.ShapeDtypeStruct((D, VN), BF16),
        in_specs=[
            pl.BlockSpec((NY * ROWS, GRAD_ROWS), lambda i: (0, i)),
            pl.BlockSpec((NY * ROWS, VN), lambda i: (0, 0)),
        ],
        out_specs=pl.BlockSpec((GRAD_ROWS, VN), lambda i: (i, 0)),
        compiler_params=pltpu.CompilerParams(vmem_limit_bytes=60 << 20),
        name="head_gradient",
    )(hidden, grad)


def local(teacher_logits, hidden, new_head, labels, map_target, map_weight):
    y = lax.axis_index("tok")
    nodes = NX * NZ * NC
    flat = map_target.reshape(1, ENT)
    owner = flat // PER - y * nodes
    match = owner == jnp.arange(nodes, dtype=jnp.int32)[:, None]
    index = jnp.arange(ENT, dtype=jnp.int32)[None, :]
    key = index * PER + flat % PER
    none = ENT * PER
    first = jnp.min(jnp.where(match, key, none), axis=1)
    last = jnp.max(jnp.where(match, key, -1), axis=1)
    first = jnp.where(first < none, first, -1)
    keys = jnp.stack([first, jnp.where(last > first, last, -1)], axis=1).reshape(2 * nodes)
    loss, grad, everyone = exchange(
        keys, labels.reshape(NY, ROWS), teacher_logits, hidden, new_head,
        map_weight.reshape(ENT, BLK, BLK),
    )
    return loss.reshape(ROWS), head_gradient(everyone, grad)


def solution(mesh):
    return jax.shard_map(
        local,
        mesh=mesh,
        in_specs=(
            P("tok", "vocab"),
            P("tok", None),
            P(None, ("tok", "vocab")),
            P(),
            P("vocab", None),
            P("vocab", None, None, None),
        ),
        out_specs=(P("tok"), P(None, ("tok", "vocab"))),
        check_vma=False,
    )
```

```python
import functools

import jax
import jax.numpy as jnp
from jax import lax
from jax.experimental import pallas as pl
from jax.experimental.pallas import tpu as pltpu
from jax.sharding import PartitionSpec as P

MESH = pl.DeviceIdType.MESH
F32 = jnp.float32
BF16 = jnp.bfloat16

NY = 4
NX = 4
NZ = 4
NC = 2
ROWS = 128
CHUNK = 64
HALF = CHUNK // 2
NU = NY * ROWS // CHUNK
BLK = 128
FAN = 4
D = 4608
HD = D // 2
VN = 1024
PER = 8
OLD = 32
ENT = OLD * FAN

FIRST = [(0, 1), (1, 0), (1, 1), (2, 0), (2, 1), (3, 0), (3, 1)]


def vocab_index(x, z, c):
    return (x * NZ + z) * NC + c


def as_row(column):
    return jnp.transpose(jnp.broadcast_to(column, (ROWS, BLK)))[0:1, :]


def as_column(row):
    return jnp.transpose(jnp.broadcast_to(row, (ROWS, BLK)))


def exchange_kernel(
    key_ref, label_ref, raw_hbm, hidden_hbm, head_hbm, weight_hbm,
    loss_ref, grad_ref, everyone_hbm,
    mask_ref, raw, prob, weight, hidden, head, logits, target, out1, in1, out2, in2, masks, mass_acc,
    log_total, mass_plus, label_at, rest,
    t1_out, t1_in, t2_out, t2_in, t3_out, t3_in,
    a1_out, a1_in, a2_out, a2_in, a3_out, a3_in,
    f1_out, f1_in, f2_out, f2_in, f3_out, f3_in,
    local_sem, raw_send, raw_recv, mask_send, mask_recv, p1_send, p1_recv, p2_send, p2_recv,
    hid_send, hid_recv, sib_send, sib_recv,
    t1_send, t1_recv, t2_send, t2_recv, t3_send, t3_recv,
    a1_send, a1_recv, a2_send, a2_recv, a3_send, a3_recv,
    f1_send, f1_recv, f2_send, f2_recv, f3_send, f3_recv,
):
    y = lax.axis_index("tok")
    v = lax.axis_index("vocab")
    x = v // (NZ * NC)
    z = (v // NC) % NZ
    c = v % NC

    def remote(src, dst, send, recv, device):
        return pltpu.make_async_remote_copy(
            src_ref=src, dst_ref=dst, send_sem=send, recv_sem=recv,
            device_id=device, device_id_type=MESH,
        )

    def along_x(step, core_step=0):
        return (y, vocab_index((x + step) % NX, z, (c + core_step) % NC))

    def along_z(step, core_step=0):
        return (y, vocab_index(x, (z + step) % NZ, (c + core_step) % NC))

    def along_y(step):
        return ((y + step) % NY, v)

    load_raw = pltpu.make_async_copy(raw_hbm, raw.at[0], local_sem.at[0])
    load_weight = pltpu.make_async_copy(weight_hbm, weight, local_sem.at[1])
    own_rows = pl.ds(pl.multiple_of(y * ROWS, ROWS), ROWS)
    load_hidden = pltpu.make_async_copy(hidden_hbm, hidden.at[own_rows], local_sem.at[2])
    load_head = pltpu.make_async_copy(head_hbm, head, local_sem.at[3])
    load_raw.start()

    barrier = pltpu.get_barrier_semaphore()
    partners = [along_x(da, dc) for da, dc in FIRST]
    partners += [along_z(da, dc) for da, dc in FIRST if da]
    partners += [along_y(step) for step in (1, 2, 3)]
    for partner in partners:
        pl.semaphore_signal(barrier, inc=1, device_id=partner, device_id_type=MESH)
    pl.semaphore_wait(barrier, len(partners))

    def first_partner(h, i):
        da, dc = FIRST[i]
        return along_x(da, dc) if h == 0 else along_z(da, dc)

    def mask_copy(h, i):
        da, dc = FIRST[i]
        c2 = (c + dc) % NC
        if h == 0:
            src = mask_ref.at[(x + da) % NX, :, c2]
        else:
            src = mask_ref.at[:, (z + da) % NZ, c2]
        return remote(src, masks.at[h, i], mask_send.at[h, i], mask_recv.at[h, i],
                      first_partner(h, i))

    def first_copy(u, h, i):
        da, dc = FIRST[i]
        c2 = (c + dc) % NC
        rows = pl.ds(h * HALF, HALF)
        if h == 0:
            src = out1.at[u, (x + da) % NX, :, c2, :, rows]
        else:
            src = out1.at[u, :, (z + da) % NZ, c2, :, rows]
        return remote(src, in1.at[u, h, i], p1_send.at[u, h, i], p1_recv.at[u, h, i],
                      first_partner(h, i))

    def second_copy(u, h, d):
        if h == 0:
            q, device = (z + d) % NZ, along_z(d)
        else:
            q, device = (x + d) % NX, along_x(d)
        return remote(out2.at[u, h, q], in2.at[u, h, d - 1], p2_send.at[u, h, d - 1],
                      p2_recv.at[u, h, d - 1], device)

    upper, lower = pl.ds(0, CHUNK), pl.ds(CHUNK, CHUNK)
    raw_copies = [
        remote(raw.at[source, rows], raw.at[into, rows], raw_send.at[i], raw_recv.at[i], along_y(d))
        for i, (source, into, rows, d) in enumerate([
            (0, 1, upper, 1), (0, 3, lower, 3), (0, 1, lower, 1), (0, 3, upper, 3),
            (1, 2, upper, 1), (3, 2, lower, 3),
        ])
    ]

    own_columns = pl.ds(pl.multiple_of(c * HD, HD), HD)

    def hidden_part(d, first=0, count=ROWS):
        start_row = ((y - d + NY) % NY) * ROWS + first
        rows = pl.ds(pl.multiple_of(start_row, CHUNK), count)
        return hidden.at[rows, own_columns]

    hidden_copies = [
        remote(hidden_part(*what), hidden_part(*what), hid_send.at[i], hid_recv.at[i], along_y(d))
        for i, (what, d) in enumerate([
            ((0, 0, CHUNK), 1), ((0, CHUNK, CHUNK), 3), ((0, CHUNK, CHUNK), 1), ((0, 0, CHUNK), 3),
            ((1, 0, CHUNK), 1), ((3, CHUNK, CHUNK), 3),
        ])
    ]

    def sibling_copy(d):
        part = hidden_part(d)
        return remote(part, part, sib_send.at[d - 1], sib_recv.at[d - 1], along_x(0, 1))

    def stage_x(out, into, send, recv):
        return [remote(out, into.at[i], send.at[i], recv.at[i], first_partner(0, i))
                for i in range(7)]

    def stage_z(out, into, send, recv):
        return [remote(out, into.at[d - 1], send.at[d - 1], recv.at[d - 1], along_z(d))
                for d in (1, 2, 3)]

    def stage_y(out, into, send, recv):
        return [remote(out, into.at[d - 1], send.at[d - 1], recv.at[d - 1], along_y(d))
                for d in (1, 2, 3)]

    pending = []

    def start(copies):
        for copy in copies:
            copy.start()
        pending.extend(copies)

    def arrived(copies):
        for copy in copies:
            copy.wait_recv()

    sublane = lax.broadcasted_iota(jnp.int32, (8, BLK), 0)

    def mask_rows(o, carry):
        for k in range(2):
            key = key_ref[o * 2 + k]
            row = jnp.where(key < 0, -1, key % PER)
            mask_ref[o // (NZ * NC), (o // NC) % NZ, o % NC, k] = (sublane == row).astype(F32)
        return carry

    load_raw.wait()
    start(raw_copies[:2])
    load_weight.start()
    load_hidden.start()
    load_head.start()

    def block_max(j, acc):
        part = raw[0, :, pl.ds(pl.multiple_of(j * BLK, BLK), BLK)].astype(F32)
        return jnp.maximum(acc, part)

    top = lax.fori_loop(1, OLD, block_max, raw[0, :, pl.ds(0, BLK)].astype(F32), unroll=4)
    top = jnp.broadcast_to(jnp.max(top, axis=1, keepdims=True), (ROWS, BLK))

    def block_sum(j, acc):
        part = raw[0, :, pl.ds(pl.multiple_of(j * BLK, BLK), BLK)].astype(F32)
        return acc + jnp.exp(part - top)

    total = lax.fori_loop(0, OLD, block_sum, jnp.zeros((ROWS, BLK), F32), unroll=4)
    total = jnp.sum(total, axis=1, keepdims=True)
    def stacked(first, second):
        return jnp.where(sublane == 0, jnp.broadcast_to(first, (8, BLK)),
                         jnp.broadcast_to(second, (8, BLK)))

    def joined(pairs):
        best = functools.reduce(jnp.maximum, [p[0:1] for p in pairs])
        mass = functools.reduce(jnp.add, [p[1:2] * jnp.exp(p[0:1] - best) for p in pairs])
        return stacked(best, mass)

    t1_out[...] = stacked(as_row(top[:, 0:1]), as_row(total))
    copies = stage_x(t1_out, t1_in, t1_send, t1_recv)
    start(copies)
    lax.fori_loop(0, NX * NZ * NC, mask_rows, 0, unroll=4)
    mask_copies = [mask_copy(h, i) for h in (0, 1) for i in range(7)]
    start(mask_copies)
    arrived(copies)
    t2_out[...] = joined([t1_out[...]] + [t1_in[i] for i in range(7)])
    copies = stage_z(t2_out, t2_in, t2_send, t2_recv)
    start(copies)
    arrived(copies)
    t3_out[...] = joined([t2_out[...]] + [t2_in[i] for i in range(3)])
    t3_copies = stage_y(t3_out, t3_in, t3_send, t3_recv)
    start(t3_copies)
    load_weight.wait()

    def contribute(g, part):
        u = g * 2 + part
        tokens = pl.ds(part * CHUNK, CHUNK)
        stats = t3_out[...] if g == 0 else t3_in[g - 1]
        best = as_column(stats[0:1])[part * CHUNK : (part + 1) * CHUNK]
        inverse = as_column(1.0 / stats[1:2])[part * CHUNK : (part + 1) * CHUNK]

        def normalise(j, carry):
            scores = raw[g, tokens, pl.ds(pl.multiple_of(j * BLK, BLK), BLK)].astype(F32)
            prob[j] = (jnp.exp(scores - best) * inverse).astype(BF16)
            return carry

        lax.fori_loop(0, OLD, normalise, 0, unroll=4)

        def slot(o, acc):
            for k in range(2):
                key = key_ref[o * 2 + k]
                e = jnp.maximum(key, 0) // PER
                filled = jnp.where(key < 0, 0.0, 1.0)
                product = jnp.dot(prob[e // FAN], weight[e], preferred_element_type=F32)
                product = product.astype(BF16)
                out1[u, o // (NZ * NC), (o // NC) % NZ, o % NC, k] = product
                acc = acc + product.astype(F32) * filled
            return acc

        acc = lax.fori_loop(0, 32, slot, jnp.zeros((CHUNK, BLK), F32), unroll=4)
        mass_acc[g, tokens] = acc
        start([first_copy(u, h, i) for i in range(7) for h in (0, 1)])

    def merge(u, h):
        arrived([first_copy(u, h, i) for i in range(7)])
        own = pl.ds(h * HALF, HALF)

        def piece(q, carry):
            sums = [jnp.zeros((HALF, BLK), F32) for _ in range(PER)]
            for i in range(8):
                for k in range(2):
                    if i < 7:
                        part, hit = in1[u, h, i, q, k], masks[h, i, q, k]
                    elif h == 0:
                        part, hit = out1[u, x, q, c, k, own], mask_ref[x, q, c, k]
                    else:
                        part, hit = out1[u, q, z, c, k, own], mask_ref[q, z, c, k]
                    part = part.astype(F32)
                    for b in range(PER):
                        sums[b] = sums[b] + part * hit[b : b + 1]
            for b in range(PER):
                out2[u, h, q, b] = sums[b].astype(BF16)
            return carry

        lax.fori_loop(0, 4, piece, 0)
        start([second_copy(u, h, d) for d in (1, 2, 3)])

    def merge_all(*units):
        for u in units:
            for h in (0, 1):
                merge(u, h)

    def group_rows(g, first=0, count=ROWS):
        start_row = ((y - g + NY) % NY) * ROWS + first
        return pl.ds(pl.multiple_of(start_row, HALF), count)

    def student(g):
        rows = group_rows(g)

        def columns_of(n, carry):
            columns = pl.ds(pl.multiple_of(n * 256, 256), 256)
            logits[rows, columns] = jnp.dot(
                hidden[rows, :], head[:, columns], preferred_element_type=F32
            )
            return carry

        lax.fori_loop(0, VN // 256, columns_of, 0)
        best = logits[rows, pl.ds(0, BLK)]
        for b in range(1, PER):
            best = jnp.maximum(best, logits[rows, pl.ds(b * BLK, BLK)])
        best = jnp.broadcast_to(jnp.max(best, axis=1, keepdims=True), (ROWS, BLK))
        acc = jnp.zeros((ROWS, BLK), F32)
        for b in range(PER):
            acc = acc + jnp.exp(logits[rows, pl.ds(b * BLK, BLK)] - best)
        a1_out[(y - g + NY) % NY] = triple(
            as_row(best[:, 0:1]),
            as_row(jnp.sum(acc, axis=1, keepdims=True)),
            as_row(jnp.sum(mass_acc[g], axis=1, keepdims=True)),
        )

    def triple(first, second, third):
        wide = [jnp.broadcast_to(r, (8, BLK)) for r in (first, second, third)]
        return jnp.where(sublane == 0, wide[0], jnp.where(sublane == 1, wide[1], wide[2]))

    base = (y * (NX * NZ * NC) + v) * VN
    lane = (lax.broadcasted_iota(jnp.int32, (HALF, BLK), 1) + base).astype(F32)

    def settle(u, h):
        arrived([second_copy(u, h, d) for d in (1, 2, 3)])
        q = z if h == 0 else x
        rows = group_rows(u // 2, (u % 2) * CHUNK + h * HALF, HALF)
        label_here = label_at[rows]
        acc = jnp.zeros((HALF, BLK), F32)
        for b in range(PER):
            here = out2[u, h, q, b].astype(F32)
            for d in range(3):
                here = here + in2[u, h, d, b].astype(F32)
            columns = pl.ds(b * BLK, BLK)
            hit = (label_here == lane + float(b * BLK)).astype(F32)
            here = here + hit
            target[rows, columns] = here
            acc = acc + here * logits[rows, columns]
        rest[rows] = acc

    def settle_all(*units):
        for u in units:
            for h in (0, 1):
                settle(u, h)

    def gradients(first, count):
        def piece(t, carry):
            rows = pl.ds(pl.multiple_of(t * 32, 32), 32)
            log_here, mass_here = log_total[rows], mass_plus[rows]
            for b in range(PER):
                columns = pl.ds(b * BLK, BLK)
                grad = mass_here * jnp.exp(logits[rows, columns] - log_here) - target[rows, columns]
                grad_ref[rows, columns] = grad.astype(BF16)
            return carry

        lax.fori_loop(first, first + count, piece, 0)

    def joined3(parts):
        best = functools.reduce(jnp.maximum, [p[0:1] for p in parts])
        exps = functools.reduce(jnp.add, [p[1:2] * jnp.exp(p[0:1] - best) for p in parts])
        mass = functools.reduce(jnp.add, [p[2:3] for p in parts])
        return triple(best, exps, mass)

    def combine(out, own, into, count):
        for q in range(NY):
            out[q] = joined3([own[q]] + [into[i, q] for i in range(count)])

    def loss_part(g):
        column = jnp.sum(rest[group_rows(g)], axis=1, keepdims=True)
        f1_out[g] = jnp.broadcast_to(as_row(column), (8, BLK))

    def loss_copy(g):
        return remote(f1_out.at[g], f1_in.at[g - 1], f1_send.at[g - 1], f1_recv.at[g - 1],
                      along_y(NY - g))

    contribute(0, 0)
    contribute(0, 1)
    arrived(raw_copies[0:2])
    start(raw_copies[2:4])
    arrived(t3_copies)
    contribute(1, 0)
    contribute(3, 1)
    arrived(mask_copies)
    merge_all(0, 1)
    arrived(raw_copies[2:4])
    start(raw_copies[4:6])
    contribute(1, 1)
    contribute(3, 0)
    load_hidden.wait()
    load_head.wait()
    start(hidden_copies[0:4])
    merge_all(2, 7)
    arrived(raw_copies[4:6])
    contribute(2, 0)
    contribute(2, 1)
    for q in range(NY):
        label_at[pl.ds(q * ROWS, ROWS)] = as_column(label_ref[pl.ds(q, 1)].astype(F32))
    student(0)
    merge_all(3, 6)
    arrived(hidden_copies[0:4])
    start(hidden_copies[4:6])
    sibling_copies = [sibling_copy(d) for d in (1, 3, 2)]
    start(sibling_copies[:2])
    arrived(sibling_copies[:2])
    student(1)
    student(3)
    arrived(hidden_copies[4:6])
    start(sibling_copies[2:])
    arrived(sibling_copies[2:])
    student(2)
    keep = pltpu.make_async_copy(hidden, everyone_hbm, local_sem.at[4])
    keep.start()

    copies = stage_y(a1_out, a1_in, a1_send, a1_recv)
    start(copies)
    settle_all(0, 1)
    arrived(copies)
    combine(a2_out, a1_out, a1_in, 3)
    copies = stage_x(a2_out, a2_in, a2_send, a2_recv)
    start(copies)
    merge_all(4)
    arrived(copies)
    combine(a3_out, a2_out, a2_in, 7)
    copies = stage_z(a3_out, a3_in, a3_send, a3_recv)
    start(copies)
    merge_all(5)
    settle_all(2, 7)
    arrived(copies)
    for q in range(NY):
        stats = joined3([a3_out[q]] + [a3_in[i, q] for i in range(3)])
        rows = pl.ds(q * ROWS, ROWS)
        log_total[rows] = as_column(stats[0:1] + jnp.log(stats[1:2]))
        mass_plus[rows] = as_column(stats[2:3] + 1.0)
        f1_out[q] = stats

    mine = f1_out[y]
    own_log = mine[0:1] + jnp.log(mine[1:2])
    own_terms = mine[2:3] * own_log + own_log
    settle_all(3, 6)
    for g in (0, 1, 3):
        loss_part(g)
    loss_copies = [loss_copy(g) for g in (1, 3, 2)]
    start(loss_copies[:2])
    settle_all(4, 5)
    loss_part(2)
    start(loss_copies[2:])
    gradients(0, 5)
    arrived(loss_copies)
    f2_out[...] = f1_out[0] + (f1_in[0] + f1_in[1] + f1_in[2])
    copies = stage_x(f2_out, f2_in, f2_send, f2_recv)
    start(copies)
    gradients(5, 6)
    arrived(copies)
    f3_out[...] = functools.reduce(jnp.add, [f2_out[...]] + [f2_in[i] for i in range(7)])
    copies = stage_z(f3_out, f3_in, f3_send, f3_recv)
    start(copies)
    gradients(11, 5)
    arrived(copies)
    everything = f3_out[...] + (f3_in[0] + f3_in[1] + f3_in[2])
    loss_ref[...] = own_terms - everything[0:1]

    keep.wait()
    for copy in pending:
        copy.wait_send()


def exchange(key, label, raw, hidden, head, weight):
    dma = pltpu.SemaphoreType.DMA
    vmem = pltpu.VMEM
    tile, quad = (8, BLK), (NY, 8, BLK)
    scratch = [
        vmem((NX, NZ, NC, 2, 8, BLK), F32),
        vmem((NY, ROWS, OLD * BLK), BF16),
        vmem((OLD, CHUNK, BLK), BF16),
        vmem((ENT, BLK, BLK), BF16),
        vmem((NY * ROWS, D), BF16),
        vmem((D, VN), BF16),
        vmem((NY * ROWS, VN), F32),
        vmem((NY * ROWS, VN), F32),
        vmem((NU, NX, NZ, NC, 2, CHUNK, BLK), BF16),
        vmem((NU, 2, 7, 4, 2, HALF, BLK), BF16),
        vmem((NU, 2, 4, PER, HALF, BLK), BF16),
        vmem((NU, 2, 3, PER, HALF, BLK), BF16),
        vmem((2, 7, 4, 2, 8, BLK), F32),
        vmem((NY, ROWS, BLK), F32),
        vmem((NY * ROWS, BLK), F32),
        vmem((NY * ROWS, BLK), F32),
        vmem((NY * ROWS, BLK), F32),
        vmem((NY * ROWS, BLK), F32),
        vmem(tile, F32), vmem((7,) + tile, F32),
        vmem(tile, F32), vmem((3,) + tile, F32),
        vmem(tile, F32), vmem((3,) + tile, F32),
        vmem(quad, F32), vmem((3,) + quad, F32),
        vmem(quad, F32), vmem((7,) + quad, F32),
        vmem(quad, F32), vmem((3,) + quad, F32),
        vmem(quad, F32), vmem((3,) + tile, F32),
        vmem(tile, F32), vmem((7,) + tile, F32),
        vmem(tile, F32), vmem((3,) + tile, F32),
        dma((5,)), dma((6,)), dma((6,)), dma((2, 7)), dma((2, 7)),
        dma((NU, 2, 7)), dma((NU, 2, 7)), dma((NU, 2, 3)), dma((NU, 2, 3)),
        dma((6,)), dma((6,)), dma((3,)), dma((3,)),
    ]
    for count in (7, 3, 3, 3, 7, 3, 3, 7, 3):
        scratch += [dma((count,)), dma((count,))]
    smem = pl.BlockSpec(memory_space=pltpu.SMEM)
    inside = pl.BlockSpec(memory_space=pltpu.VMEM)
    outside = pl.BlockSpec(memory_space=pl.ANY)
    return pl.pallas_call(
        exchange_kernel,
        out_shape=(
            jax.ShapeDtypeStruct((1, ROWS), F32),
            jax.ShapeDtypeStruct((NY * ROWS, VN), BF16),
            jax.ShapeDtypeStruct((NY * ROWS, D), BF16),
        ),
        in_specs=[smem, inside] + [outside] * 4,
        out_specs=(inside, inside, outside),
        scratch_shapes=scratch,
        compiler_params=pltpu.CompilerParams(
            collective_id=0, has_side_effects=True, vmem_limit_bytes=60 << 20
        ),
        name="exchange",
    )(key, label, raw, hidden, head, weight)


GRAD_ROWS = 1536


def grad_kernel(hidden_ref, grad_ref, out_ref):
    out_ref[...] = lax.dot_general(
        hidden_ref[...], grad_ref[...], (((0,), (0,)), ((), ())), preferred_element_type=F32
    ).astype(BF16)


def head_gradient(hidden, grad):
    return pl.pallas_call(
        grad_kernel,
        grid=(D // GRAD_ROWS,),
        out_shape=jax.ShapeDtypeStruct((D, VN), BF16),
        in_specs=[
            pl.BlockSpec((NY * ROWS, GRAD_ROWS), lambda i: (0, i)),
            pl.BlockSpec((NY * ROWS, VN), lambda i: (0, 0)),
        ],
        out_specs=pl.BlockSpec((GRAD_ROWS, VN), lambda i: (i, 0)),
        compiler_params=pltpu.CompilerParams(vmem_limit_bytes=60 << 20),
        name="head_gradient",
    )(hidden, grad)


def local(teacher_logits, hidden, new_head, labels, map_target, map_weight):
    y = lax.axis_index("tok")
    nodes = NX * NZ * NC
    flat = map_target.reshape(1, ENT)
    owner = flat // PER - y * nodes
    match = owner == jnp.arange(nodes, dtype=jnp.int32)[:, None]
    index = jnp.arange(ENT, dtype=jnp.int32)[None, :]
    key = index * PER + flat % PER
    none = ENT * PER
    first = jnp.min(jnp.where(match, key, none), axis=1)
    last = jnp.max(jnp.where(match, key, -1), axis=1)
    first = jnp.where(first < none, first, -1)
    keys = jnp.stack([first, jnp.where(last > first, last, -1)], axis=1).reshape(2 * nodes)
    loss, grad, everyone = exchange(
        keys, labels.reshape(NY, ROWS), teacher_logits, hidden, new_head,
        map_weight.reshape(ENT, BLK, BLK),
    )
    return loss.reshape(ROWS), head_gradient(everyone, grad)


def solution(mesh):
    return jax.shard_map(
        local,
        mesh=mesh,
        in_specs=(
            P("tok", "vocab"),
            P("tok", None),
            P(None, ("tok", "vocab")),
            P(),
            P("vocab", None),
            P("vocab", None, None, None),
        ),
        out_specs=(P("tok"), P(None, ("tok", "vocab"))),
        check_vma=False,
    )
```
